32 devices in a mesh: dp: 16 (over z, y, x), seq: 2 (over core).
Axes of the slice: x: 2, y: 2, z: 4, core: 2. Of those that a mesh axis runs over, the one named last changes fastest.
Arguments:
- hidden_in: bfloat16 [16, 1024, 768], P('dp', 'seq'), may hold values from -8 to 8
- out_grad: bfloat16 [16, 1024, 768], P('dp', 'seq'), may hold values from -6 to 6
- segments: int32 [16, 1024], P('dp'), may hold values from 0 to 16383, as said below
- qkv_weight: bfloat16 [768, 2304], replicated, may hold values from -0.21875 to 0.21875
- out_weight: bfloat16 [768, 768], replicated, may hold values from -0.875 to 0.875
- ffn_in: bfloat16 [768, 3072], replicated, may hold values from -0.21875 to 0.21875
- ffn_out: bfloat16 [3072, 768], replicated, may hold values from -0.109375 to 0.109375
- first_down: bfloat16 [768, 64], replicated, may hold values from -0.21875 to 0.21875
- first_down_bias: float32 [64], replicated, may hold values from -3 to 3
- first_up: bfloat16 [64, 768], replicated, may hold values from -0.359375 to 0.359375
- first_up_bias: float32 [768], replicated, may hold values from -1.8 to 1.8
- second_down: bfloat16 [768, 64], replicated, may hold values from -0.21875 to 0.21875
- second_down_bias: float32 [64], replicated, may hold values from -3 to 3
- second_up: bfloat16 [64, 768], replicated, may hold values from -0.359375 to 0.359375
- second_up_bias: float32 [768], replicated, may hold values from -1.8 to 1.8
- norm1_gain: float32 [768], replicated, may hold values from 0.5 to 1.5
- norm1_bias: float32 [768], replicated, may hold values from -1.8 to 1.8
- norm2_gain: float32 [768], replicated, may hold values from 0.5 to 1.5
- norm2_bias: float32 [768], replicated, may hold values from -1.8 to 1.8
Outputs:
- layer_out: bfloat16 [16, 1024, 768], P('dp', 'seq')
- input_grad: bfloat16 [16, 1024, 768], P('dp', 'seq')
- first_down_grad: float32 [768, 64], replicated
- first_down_bias_grad: float32 [64], replicated
- first_up_grad: float32 [64, 768], replicated
- first_up_bias_grad: float32 [768], replicated
- second_down_grad: float32 [768, 64], replicated
- second_down_bias_grad: float32 [64], replicated
- second_up_grad: float32 [64, 768], replicated
- second_up_bias_grad: float32 [768], replicated
- norm1_gain_grad: float32 [768], replicated
- norm1_bias_grad: float32 [768], replicated
- norm2_gain_grad: float32 [768], replicated
- norm2_bias_grad: float32 [768], replicated
- first_ratio: float32 [], replicated
- second_ratio: float32 [], replicated
The draws below stay inside these ranges and needn't reach their ends.
Inputs may be any that keep to these rules, and one draw needn't show every extreme that they name: segments[s, p] is s * 1024 plus the first position of the document that holds position p of sequence s, so it never falls along a row and is equal exactly inside a document; one document of each sequence holds the positions 256 to 768; the last position of every sequence is a document of its own.
All inputs are finite; a program needn't handle non-finite values.
Results may differ from the reference program's by a relative error of at most 0.014.
The reference program's roundings to bfloat16 on the way count: a program that leaves them out, or rounds other values in their place, can miss the bound.
Values may be sent and summed in bfloat16 or wider, within the bound.
No kernel may reach another device: no remote copies, remote signals or barrier semaphores. Data moves between devices by JAX's collectives and lax.ppermute only.
A program may use at most 192 MiB of HBM per device.

```python
import math
import jax
import jax.numpy as jnp
from jax import lax

D = 768
HEADS = 12
FF = 3072
ADAPT = 64
LEN = 1024
SEQ_COUNT = 16


def draw_segments(key, part):
    key = jax.random.fold_in(key, 11)
    spacing = max(4, LEN // 24)
    place = lax.broadcasted_iota(jnp.int32, (SEQ_COUNT, LEN), 1)
    row_index = lax.broadcasted_iota(jnp.int32, (SEQ_COUNT, LEN), 0)
    marks = (jax.random.randint(key, (SEQ_COUNT, LEN), 0, spacing) == 0) | (place == LEN - 1)
    inner = (place >= LEN // 4) & (place <= 3 * LEN // 4)
    starts = jnp.where(marks & (place > 0) & jnp.logical_not(inner), place, 0)
    starts = lax.cummax(starts, axis=1)
    return (starts + row_index * LEN).astype(jnp.int32)


def draw_hidden_in(key, part):
    key = jax.random.fold_in(key, 13)
    order = lax.broadcasted_iota(jnp.float32, (SEQ_COUNT, 1, 1), 0) / max(SEQ_COUNT - 1, 1)
    values = jnp.clip(jax.random.normal(key, (SEQ_COUNT, LEN, D), jnp.float32), -4.0, 4.0)
    level = 0.6 * jnp.exp(order * jnp.log(3.0))
    return (values * level).astype(jnp.bfloat16)


def shard_levels(own_key, dims, cuts, least, top_value):
    def one(axis_at, parts):
        draws = jax.random.uniform(jax.random.fold_in(jax.random.fold_in(own_key, 6), axis_at), (parts,), jnp.float32, least / len(cuts), top_value / len(cuts))
        return jnp.repeat(jnp.exp(draws), dims[axis_at] // parts).reshape((-1,) + (1,) * (len(dims) - axis_at - 1))

    loudness = one(*cuts[0])
    for cut in cuts[1:]:
        loudness = loudness * one(*cut)
    return loudness


def bell_draw(key, shape, scale, reach, split=(), dtype=jnp.bfloat16):
    values = scale * jax.random.normal(key, shape, jnp.float32)
    if split:
        values = values * shard_levels(key, shape, split, -0.22, 0.18)
    return jnp.clip(values, -reach, reach).astype(dtype)


def setup_inputs(seed: int = 0) -> dict:
    streams_of = jax.random.split(jax.random.key(seed), 20)
    hidden_in = draw_hidden_in(jax.random.fold_in(streams_of[19], 71), 0)
    out_grad = bell_draw(streams_of[1], (SEQ_COUNT, LEN, D), 1.0, 6.0, ((0, 16), (1, 2)))
    segments = draw_segments(jax.random.fold_in(streams_of[19], 71), 0)
    qkv_weight = bell_draw(streams_of[3], (D, 3 * D), D ** -0.5, 0.21875)
    out_weight = bell_draw(streams_of[4], (D, D), (D // 16) ** -0.5, 0.875)
    ffn_in = bell_draw(streams_of[5], (D, FF), D ** -0.5, 0.21875)
    ffn_out = bell_draw(streams_of[6], (FF, D), FF ** -0.5, 0.109375)
    first_down = bell_draw(streams_of[7], (D, ADAPT), D ** -0.5, 0.21875)
    first_down_bias = bell_draw(streams_of[8], (ADAPT,), 0.5, 3.0, (), jnp.float32)
    first_up = bell_draw(streams_of[9], (ADAPT, D), 0.06, 0.359375)
    first_up_bias = bell_draw(streams_of[10], (D,), 0.3, 1.8, (), jnp.float32)
    second_down = bell_draw(streams_of[11], (D, ADAPT), D ** -0.5, 0.21875)
    second_down_bias = bell_draw(streams_of[12], (ADAPT,), 0.5, 3.0, (), jnp.float32)
    second_up = bell_draw(streams_of[13], (ADAPT, D), 0.06, 0.359375)
    second_up_bias = bell_draw(streams_of[14], (D,), 0.3, 1.8, (), jnp.float32)
    norm1_gain = jnp.clip(1.0 + 0.1 * jax.random.normal(streams_of[15], (D,), jnp.float32), 0.5, 1.5)
    norm1_bias = bell_draw(streams_of[16], (D,), 0.3, 1.8, (), jnp.float32)
    norm2_gain = jnp.clip(1.0 + 0.1 * jax.random.normal(streams_of[17], (D,), jnp.float32), 0.5, 1.5)
    norm2_bias = bell_draw(streams_of[18], (D,), 0.3, 1.8, (), jnp.float32)
    return dict(hidden_in=hidden_in, out_grad=out_grad, segments=segments, qkv_weight=qkv_weight, out_weight=out_weight, ffn_in=ffn_in, ffn_out=ffn_out, first_down=first_down, first_down_bias=first_down_bias, first_up=first_up, first_up_bias=first_up_bias, second_down=second_down, second_down_bias=second_down_bias, second_up=second_up, second_up_bias=second_up_bias, norm1_gain=norm1_gain, norm1_bias=norm1_bias, norm2_gain=norm2_gain, norm2_bias=norm2_bias)


@jax.custom_vjp
def low(v):
    return lax.optimization_barrier(v.astype(jnp.bfloat16)).astype(jnp.float32)

@jax.custom_vjp
def low_back(v):
    return v

def low_keep(v):
    return (low(v), None)

def low_pass(kept, grad):
    return (grad,)

def back_keep(v):
    return (v, None)

def back_low(kept, grad):
    return (low(grad),)
low.defvjp(low_keep, low_pass)
low_back.defvjp(back_keep, back_low)

def matmul(left, right):
    return jnp.dot(left, right, precision=lax.Precision.HIGHEST, preferred_element_type=jnp.float32)

def gelu_exact(value):
    return jax.nn.gelu(value, approximate=False)

def layer_norm(resid, gain, bias):
    center = resid - lax.optimization_barrier(jnp.mean(resid, axis=-1, keepdims=True))
    spread = lax.optimization_barrier(jnp.mean(center * center, axis=-1, keepdims=True))
    return center * lax.rsqrt(spread + 1e-12) * gain + bias

def adapter(inputs, w_down, b_down, w_up, b_up):
    pre = low_back(matmul(inputs, w_down) + b_down)
    hidden = low(gelu_exact(pre))
    return low_back(matmul(hidden, w_up) + b_up)

def forward(tokens, seg, frozen, trained):
    w_qkv, w_out, w_in, w_back = frozen
    d1, bd1, u1, bu1, d2, bd2, u2, bu2, g1, b1, g2, b2 = trained
    length = tokens.shape[0]
    width = tokens.shape[1]
    head_dim = width // HEADS
    scale = 1.0 / math.sqrt(head_dim)
    qkv = low(low_back(matmul(tokens, w_qkv)))
    query = qkv[:, :width].reshape(length, HEADS, head_dim)
    keys = qkv[:, width:2 * width].reshape(length, HEADS, head_dim)
    values = qkv[:, 2 * width:].reshape(length, HEADS, head_dim)
    scores = jnp.einsum('qhd,khd->hqk', query, keys, precision=lax.Precision.HIGHEST) * scale
    scores = low_back(scores)
    same = seg[:, None] == seg[None, :]
    scores = jnp.where(same[None], scores, -1000000000.0)
    probs = low(jax.nn.softmax(scores, axis=-1))
    context = jnp.einsum('hqk,khd->qhd', probs, values, precision=lax.Precision.HIGHEST)
    context = low(low_back(context.reshape(length, width)))
    attn = low(low_back(matmul(context, w_out)))
    branch1 = adapter(attn, d1, bd1, u1, bu1)
    normed = layer_norm(tokens + attn + branch1, g1, b1)
    ffn_pre = low_back(matmul(low(normed), w_in))
    ffn_act = low(gelu_exact(ffn_pre))
    ffn_post = low(low_back(matmul(ffn_act, w_back)))
    branch2 = adapter(ffn_post, d2, bd2, u2, bu2)
    out = layer_norm(normed + ffn_post + branch2, g2, b2)
    sums = (jnp.sum(branch1 * branch1), jnp.sum(tokens * tokens), jnp.sum(branch2 * branch2), jnp.sum(normed * normed))
    return (out, sums)

def reference(hidden_in, out_grad, segments, qkv_weight, out_weight, ffn_in, ffn_out, first_down, first_down_bias, first_up, first_up_bias, second_down, second_down_bias, second_up, second_up_bias, norm1_gain, norm1_bias, norm2_gain, norm2_bias):
    frozen = (qkv_weight.astype(jnp.float32), out_weight.astype(jnp.float32), ffn_in.astype(jnp.float32), ffn_out.astype(jnp.float32))
    trained = (first_down.astype(jnp.float32), first_down_bias.astype(jnp.float32), first_up.astype(jnp.float32), first_up_bias.astype(jnp.float32), second_down.astype(jnp.float32), second_down_bias.astype(jnp.float32), second_up.astype(jnp.float32), second_up_bias.astype(jnp.float32), norm1_gain.astype(jnp.float32), norm1_bias.astype(jnp.float32), norm2_gain.astype(jnp.float32), norm2_bias.astype(jnp.float32))

    def one_sequence(carry, item):
        tokens_bf, grad_bf, seg = item
        tokens = tokens_bf.astype(jnp.float32)

        def local_forward(tok, params):
            return forward(tok, seg, frozen, params)
        (out, sums), backward = jax.vjp(local_forward, tokens, trained)
        nothing = (jnp.zeros((), jnp.float32), jnp.zeros((), jnp.float32), jnp.zeros((), jnp.float32), jnp.zeros((), jnp.float32))
        d_tokens, d_params = backward((grad_bf.astype(jnp.float32), nothing))
        grads, totals = carry
        grads = jax.tree.map(lambda a, b: a + b, grads, d_params)
        totals = jax.tree.map(lambda a, b: a + b, totals, sums)
        return ((grads, totals), (out.astype(jnp.bfloat16), d_tokens.astype(jnp.bfloat16)))
    start = (jax.tree.map(jnp.zeros_like, trained), (jnp.zeros((), jnp.float32), jnp.zeros((), jnp.float32), jnp.zeros((), jnp.float32), jnp.zeros((), jnp.float32)))
    (grads, totals), (outs, d_inputs) = lax.scan(one_sequence, start, (hidden_in, out_grad, segments))
    first_ratio = jnp.sqrt(totals[0]) / jnp.sqrt(totals[1])
    second_ratio = jnp.sqrt(totals[2]) / jnp.sqrt(totals[3])
    return (outs, d_inputs, grads[0], grads[1], grads[2], grads[3], grads[4], grads[5], grads[6], grads[7], grads[8], grads[9], grads[10], grads[11], first_ratio, second_ratio)
```

```python
import functools
import math

import jax
import jax.numpy as jnp
from jax import lax
from jax.experimental import pallas as pl
from jax.experimental.pallas import tpu as pltpu
from jax.sharding import PartitionSpec as P

HEADS = 12
F32 = jnp.float32
BF16 = jnp.bfloat16
LOG2E = math.log2(math.e)
MASKED = -1.0e9
MIB = 1024 * 1024
LANES = 128
TILE = 32

NN = (((1,), (0,)), ((), ()))
NT = (((1,), (1,)), ((), ()))
TN = (((0,), (0,)), ((), ()))


def mm(left, right, dims=NN):
    return lax.dot_general(left, right, dims, preferred_element_type=F32)


def gelu_pair(v):
    cdf = 0.5 + 0.5 * lax.erf(v * math.sqrt(0.5))
    bell = jnp.exp2(v * v * (-0.5 * LOG2E))
    return v * cdf, cdf + v * bell * (1.0 / math.sqrt(2.0 * math.pi))


def row(ref):
    return ref[...].reshape(1, -1)


def rows_sum(value):
    return jnp.sum(value, axis=0, keepdims=True)


def lanes_mean(value):
    return jnp.mean(value, axis=-1, keepdims=True)


def fold(value):
    return jnp.sum(value.reshape(-1, 8, value.shape[-1]), axis=0)


def each_tile(rows, tile, body, sums):
    for at in range(0, rows, tile):
        sums = body(slice(at, at + tile), sums)
    return sums


def total(value):
    return jnp.sum(rows_sum(value), axis=1, keepdims=True)


def norm_forward(resid):
    center = resid - lanes_mean(resid)
    rstd = lax.rsqrt(lanes_mean(center * center) + 1e-12)
    return center * rstd, rstd


def packed_rows(adapt, width):
    rows = 4 * adapt * (width // LANES) + 6 * (width // LANES) + 2
    return -(-rows // 32) * 32


def put_packed(ref, number, value):
    rows, width = value.shape
    for i in range(width // LANES):
        at = (number * (width // LANES) + i) * rows
        ref[at : at + rows] = value[:, i * LANES : (i + 1) * LANES]


def norm_backward(xhat, rstd, dxhat):
    return rstd * (dxhat - lanes_mean(dxhat) - xhat * lanes_mean(dxhat * xhat))


def head_lanes(pair, which, head_dim):
    lane = lax.broadcasted_iota(jnp.int32, pair.shape, 1)
    keep = (lane < head_dim) if which == 0 else (lane >= head_dim)
    return jnp.where(keep, pair, jnp.zeros_like(pair))


def head_rows(pair, which, head_dim):
    part = pair[which * head_dim : (which + 1) * head_dim]
    blank = jnp.zeros_like(part)
    return jnp.concatenate([part, blank] if which == 0 else [blank, part], axis=0)


def params(vmem=20, **more):
    return pltpu.CompilerParams(vmem_limit_bytes=vmem * MIB, **more)


def cost(flops, moved, exps=0):
    return pl.CostEstimate(flops=int(flops), bytes_accessed=int(moved), transcendentals=int(exps))


def stay(*arrays):
    return [pltpu.with_memory_space_constraint(x, pltpu.HBM) for x in arrays]


def qkv_kernel(x_hbm, w_hbm, kv_ref, q_ref, x_ref, w_ref, sem):
    width = x_ref.shape[1]
    load_x = pltpu.make_async_copy(x_hbm, x_ref, sem.at[3])
    load_x.start()
    loads = []
    for i, part in enumerate((1, 2, 0)):
        span = pl.ds(part * width, width)
        loads.append(pltpu.make_async_copy(w_hbm.at[:, span], w_ref.at[i], sem.at[i]))
        loads[-1].start()
    load_x.wait()
    for i in range(2):
        loads[i].wait()
        kv_ref[:, i * width : (i + 1) * width] = mm(x_ref[...], w_ref[i]).astype(BF16)
    loads[2].wait()
    q_ref[...] = mm(x_ref[...], w_ref[2]).astype(BF16)


VMEM = pl.BlockSpec(memory_space=pltpu.VMEM)
SMEM = pl.BlockSpec(memory_space=pltpu.SMEM)
HBM = pl.BlockSpec(memory_space=pl.ANY)


def project(x, qkv_weight):
    rows, width = x.shape
    return pl.pallas_call(
        qkv_kernel,
        in_specs=[HBM, HBM],
        out_specs=[VMEM] * 2,
        out_shape=[
            jax.ShapeDtypeStruct((rows, 2 * width), BF16),
            jax.ShapeDtypeStruct((rows, width), BF16),
        ],
        scratch_shapes=[
            pltpu.VMEM((rows, width), BF16),
            pltpu.VMEM((3, width, width), BF16),
            pltpu.SemaphoreType.DMA((4,)),
        ],
        compiler_params=params(16),
        cost_estimate=cost(6 * rows * width * width, 6 * width * width),
        name="project",
    )(*stay(x, qkv_weight))


def fill_bias(bias_ref, ids_ref, key_side, query_side):
    half = bias_ref.shape[0]
    keys = ids_ref[:, pl.ds(pl.multiple_of(key_side * half, half), half)].astype(F32)
    queries = ids_ref[:, pl.ds(pl.multiple_of(query_side * half, half), half)].astype(F32)
    column = jnp.broadcast_to(keys, (LANES, half)).T
    for lo in range(0, half, LANES):
        bias_ref[:, lo : lo + LANES] = jnp.where(column == queries[:, lo : lo + LANES], 0.0, MASKED)


def softmax_head(level_ref, bias_ref, unit, e_ref, floor=None):
    rows, columns = level_ref.shape
    peak = None
    for r in range(0, rows, TILE):
        level = level_ref[r : r + TILE] * unit + bias_ref[r : r + TILE]
        level_ref[r : r + TILE] = level
        part = jnp.max(level.reshape(-1, 8, columns), axis=0)
        peak = part if peak is None else jnp.maximum(peak, part)
    top = jnp.max(peak, axis=0, keepdims=True)
    if floor is not None:
        top = jnp.maximum(top, floor)
    mass = None
    for r in range(0, rows, TILE):
        e = jnp.exp2(level_ref[r : r + TILE] - top)
        e_ref[r : r + TILE] = e.astype(BF16)
        mass = fold(e) if mass is None else mass + fold(e)
    return top, rows_sum(mass)


def lanes(pair, base=0):
    return slice(base + pair * LANES, base + (pair + 1) * LANES)


def score_head(level_ref, q_ref, kv_ref, head):
    at = lanes(head // 2)
    queries = head_rows(q_ref[:, at].T, head % 2, LANES // 2)
    level_ref[...] = mm(kv_ref[:, at], queries)


def near_kernel(me_ref, q_ref, kv_ref, ids_ref, ct_ref, st_ref, e_ref, bias_ref, level_ref):
    side = lax.rem(me_ref[0], 2)
    fill_bias(bias_ref, ids_ref, side, side)
    width = q_ref.shape[1]
    head_dim = LANES // 2
    unit = LOG2E / math.sqrt(head_dim)
    score_head(level_ref.at[0], q_ref, kv_ref, 0)
    for head in range(HEADS):
        if head + 1 < HEADS:
            score_head(level_ref.at[(head + 1) % 2], q_ref, kv_ref, head + 1)
        pair, which = head // 2, head % 2
        top, mass = softmax_head(level_ref.at[head % 2], bias_ref, unit, e_ref.at[head])
        values = kv_ref[:, lanes(pair, width)].T[which * head_dim : (which + 1) * head_dim]
        ct_ref[head * head_dim : (head + 1) * head_dim] = mm(values, e_ref[head])
        st_ref[pair, which : which + 1] = top
        st_ref[pair, 2 + which : 3 + which] = mass


def attend_near(me, q, kv, ids):
    rows, width = q.shape
    pairs = width // LANES
    return pl.pallas_call(
        near_kernel,
        in_specs=[SMEM] + [VMEM] * 3,
        out_specs=[VMEM] * 3,
        out_shape=[
            jax.ShapeDtypeStruct((width, rows), F32),
            jax.ShapeDtypeStruct((pairs, 8, rows), F32),
            jax.ShapeDtypeStruct((HEADS, rows, rows), BF16),
        ],
        scratch_shapes=[pltpu.VMEM((rows, rows), F32), pltpu.VMEM((2, rows, rows), F32)],
        compiler_params=params(14),
        cost_estimate=cost(8 * rows * rows * width, 3 * HEADS * rows * rows, HEADS * rows * rows),
        name="attend_near",
    )(me, q, kv, ids)


def far_kernel(
    me_ref,
    q_ref,
    came_hbm,
    ids_ref,
    cn_ref,
    sn_ref,
    kv_ref,
    c_ref,
    ct_ref,
    st_ref,
    e_ref,
    bias_ref,
    level_ref,
    sem,
):
    width = q_ref.shape[1]
    loads = []
    for i in range(2):
        span = pl.ds(i * width, width)
        loads.append(pltpu.make_async_copy(came_hbm.at[:, span], kv_ref.at[:, span], sem.at[i]))
        loads[i].start()
    side = lax.rem(me_ref[0], 2)
    fill_bias(bias_ref, ids_ref, 1 - side, side)
    head_dim = LANES // 2
    unit = LOG2E / math.sqrt(head_dim)
    loads[0].wait()
    loads[1].wait()
    score_head(level_ref.at[0], q_ref, kv_ref, 0)
    for head in range(HEADS):
        if head + 1 < HEADS:
            score_head(level_ref.at[(head + 1) % 2], q_ref, kv_ref, head + 1)
        pair, which = head // 2, head % 2
        near_top = sn_ref[pair, which : which + 1]
        near_mass = sn_ref[pair, 2 + which : 3 + which]
        top, mass = softmax_head(level_ref.at[head % 2], bias_ref, unit, e_ref.at[head], near_top)
        near_part = jnp.exp2(near_top - top)
        inverse = 1.0 / (mass + near_mass * near_part)
        values = kv_ref[:, lanes(pair, width)].T[which * head_dim : (which + 1) * head_dim]
        rows = slice(head * head_dim, (head + 1) * head_dim)
        ct_ref[rows] = (mm(values, e_ref[head]) + cn_ref[rows] * near_part) * inverse
        st_ref[pair, which : which + 1] = near_part * inverse
        st_ref[pair, 2 + which : 3 + which] = inverse
        if which:
            c_ref[:, lanes(pair)] = ct_ref[lanes(pair)].astype(BF16).T


def attend_far(me, q, came, ids, near_ct, near_st):
    rows, width = q.shape
    pairs = width // LANES
    return pl.pallas_call(
        far_kernel,
        in_specs=[SMEM, VMEM, HBM] + [VMEM] * 3,
        out_specs=[VMEM] * 5,
        out_shape=[
            jax.ShapeDtypeStruct((rows, 2 * width), BF16),
            jax.ShapeDtypeStruct((rows, width), BF16),
            jax.ShapeDtypeStruct((width, rows), F32),
            jax.ShapeDtypeStruct((pairs, 8, rows), F32),
            jax.ShapeDtypeStruct((HEADS, rows, rows), BF16),
        ],
        scratch_shapes=[
            pltpu.VMEM((rows, rows), F32),
            pltpu.VMEM((2, rows, rows), F32),
            pltpu.SemaphoreType.DMA((2,)),
        ],
        compiler_params=params(14),
        cost_estimate=cost(6 * rows * rows * width, 3 * HEADS * rows * rows, HEADS * rows * rows),
        name="attend_far",
    )(me, q, came, ids, near_ct, near_st)


def middle_kernel(
    me_ref,
    x_ref,
    og_ref,
    c_ref,
    wo_ref,
    fi_ref,
    fo_ref,
    d1_ref,
    bd1_ref,
    u1_ref,
    bu1_ref,
    d2_ref,
    bd2_ref,
    u2_ref,
    bu2_ref,
    g1_ref,
    b1_ref,
    g2_ref,
    b2_ref,
    out_hbm,
    df_ref,
    dc_ref,
    *rest,
):
    own_ref, other_ref, *scratch = rest
    (
        out_ref,
        sem,
        grad_ref,
        attn_ref,
        branch_ref,
        xhat_ref,
        rstd_ref,
        normed_ref,
        nb_ref,
        post_ref,
        pre_ref,
        act_ref,
        slope_ref,
    ) = scratch
    db_ref, acc_ref = nb_ref, branch_ref

    rows, width = x_ref.shape
    ff = fi_ref.shape[1]
    wide = pre_ref.shape[2]
    chunks = ff // wide
    none = jnp.zeros((8, width), F32)

    attn_ref[...] = mm(c_ref[...], wo_ref[...]).astype(BF16)
    hidden, slope_one = gelu_pair(mm(attn_ref[...], d1_ref[...], NT) + row(bd1_ref))
    hidden_one = hidden.astype(BF16)
    branch_ref[...] = mm(hidden_one, u1_ref[...])

    def first_norm(at, sums):
        x = x_ref[at].astype(F32)
        branch = branch_ref[at] + row(bu1_ref)
        xhat, rstd = norm_forward(x + attn_ref[at].astype(F32) + branch)
        normed = xhat * row(g1_ref) + row(b1_ref)
        xhat_ref[at] = xhat
        rstd_ref[at] = rstd
        normed_ref[at] = normed
        nb_ref[at] = normed.astype(BF16)
        terms = (branch * branch, x * x, normed * normed)
        return tuple(a + fold(b) for a, b in zip(sums, terms))

    branch_sq, input_sq, normed_sq = map(total, each_tile(rows, 32, first_norm, (none,) * 3))

    pre_ref[0] = mm(nb_ref[...], fi_ref[:, :wide])
    for j in range(chunks):
        if j + 1 < chunks:
            pre_ref[(j + 1) % 2] = mm(nb_ref[...], fi_ref[:, (j + 1) * wide : (j + 2) * wide])
        for r in range(0, rows, 16):
            act, slope = gelu_pair(pre_ref[j % 2, r : r + 16])
            act_ref[j % 2, r : r + 16] = act.astype(BF16)
            slope_ref[r : r + 16, j * wide : (j + 1) * wide] = slope.astype(BF16)
        part = mm(act_ref[j % 2], fo_ref[j * wide : (j + 1) * wide])
        if j == 0:
            acc_ref[...] = part
        else:
            acc_ref[...] += part

    post_ref[...] = acc_ref[...].astype(BF16)
    hidden, slope_two = gelu_pair(mm(post_ref[...], d2_ref[...], NT) + row(bd2_ref))
    hidden_two = hidden.astype(BF16)
    branch_ref[...] = mm(hidden_two, u2_ref[...])

    def second_norm(at, sums):
        branch = branch_ref[at] + row(bu2_ref)
        xhat, rstd = norm_forward(normed_ref[at] + post_ref[at].astype(F32) + branch)
        out_ref[at] = (xhat * row(g2_ref) + row(b2_ref)).astype(BF16)
        og = og_ref[at].astype(F32)
        d_second = norm_backward(xhat, rstd, og * row(g2_ref))
        d_branch = d_second.astype(BF16)
        normed_ref[at] = d_second
        db_ref[at] = d_branch
        terms = (branch * branch, og * xhat, og, d_branch.astype(F32))
        return tuple(a + fold(b) for a, b in zip(sums, terms))

    second_sq, gain2, bias2, up_bias2 = each_tile(rows, 32, second_norm, (none,) * 4)
    save = pltpu.make_async_copy(out_ref, out_hbm, sem)
    save.start()
    second_sq = total(second_sq)
    gain2, bias2, up_bias2 = map(rows_sum, (gain2, bias2, up_bias2))
    put_packed(grad_ref, 0, mm(hidden_two, db_ref[...], TN))
    d_pre = (mm(db_ref[...], u2_ref[...], NT) * slope_two).astype(BF16)
    put_packed(grad_ref, 1, mm(d_pre, post_ref[...], TN))
    down_bias2 = rows_sum(d_pre.astype(F32))
    post_ref[...] = (normed_ref[...] + mm(d_pre, d2_ref[...])).astype(BF16)

    pre_ref[0] = mm(post_ref[...], fo_ref[:wide], NT)
    for j in range(chunks):
        if j + 1 < chunks:
            pre_ref[(j + 1) % 2] = mm(post_ref[...], fo_ref[(j + 1) * wide : (j + 2) * wide], NT)
        for r in range(0, rows, 16):
            slope = slope_ref[r : r + 16, j * wide : (j + 1) * wide].astype(F32)
            act_ref[j % 2, r : r + 16] = (pre_ref[j % 2, r : r + 16] * slope).astype(BF16)
        part = mm(act_ref[j % 2], fi_ref[:, j * wide : (j + 1) * wide], NT)
        if j == 0:
            acc_ref[...] = part
        else:
            acc_ref[...] += part

    def first_back(at, sums):
        d_normed = normed_ref[at] + acc_ref[at]
        xhat = xhat_ref[at]
        d_first = norm_backward(xhat, rstd_ref[at], d_normed * row(g1_ref))
        d_branch = d_first.astype(BF16)
        df_ref[at] = d_first
        db_ref[at] = d_branch
        terms = (d_normed * xhat, d_normed, d_branch.astype(F32))
        return tuple(a + fold(b) for a, b in zip(sums, terms))

    gain1, bias1, up_bias1 = map(rows_sum, each_tile(rows, 32, first_back, (none,) * 3))
    put_packed(grad_ref, 2, mm(hidden_one, db_ref[...], TN))
    d_pre = (mm(db_ref[...], u1_ref[...], NT) * slope_one).astype(BF16)
    put_packed(grad_ref, 3, mm(d_pre, attn_ref[...], TN))
    down_bias1 = rows_sum(d_pre.astype(F32))
    d_attn = (df_ref[...] + mm(d_pre, d1_ref[...])).astype(BF16)
    dc_ref[...] = mm(d_attn, wo_ref[...], NT).astype(BF16)

    lane = lax.broadcasted_iota(jnp.int32, (1, LANES), 1)
    sums = jnp.where(lane == 0, branch_sq, 0.0)
    sums = jnp.where(lane == 1, input_sq, sums)
    sums = jnp.where(lane == 2, second_sq, sums)
    sums = jnp.where(lane == 3, normed_sq, sums)
    at = 4 * d1_ref.shape[0] * (width // LANES)
    grad_ref[at:] = jnp.zeros((grad_ref.shape[0] - at, LANES), F32)
    for vector in (up_bias1, up_bias2, gain1, bias1, gain2, bias2):
        for lo in range(0, width, LANES):
            grad_ref[at : at + 1] = vector[:, lo : lo + LANES]
            at += 1
    grad_ref[at : at + 1] = jnp.concatenate([down_bias1, down_bias2], axis=1)
    grad_ref[at + 1 : at + 2] = sums
    save.wait()
    half = grad_ref.shape[0] // 2
    side = lax.rem(me_ref[0], 2)
    own_ref[...] = grad_ref[pl.ds(pl.multiple_of(side * half, half), half), :]
    other_ref[...] = grad_ref[pl.ds(pl.multiple_of((1 - side) * half, half), half), :].astype(BF16)


def middle(x, og, ctx, out_weight, ffn_in, ffn_out, small, me, packed):
    rows, width = x.shape
    ff = ffn_in.shape[1]
    adapt = small[0].shape[0]
    vmem = pl.BlockSpec(memory_space=pltpu.VMEM)
    smem = pl.BlockSpec(memory_space=pltpu.SMEM)
    return pl.pallas_call(
        middle_kernel,
        in_specs=[smem] + [vmem] * (6 + len(small)),
        out_specs=[HBM] + [vmem] * 4,
        out_shape=[
            pltpu.HBM((rows, width), BF16),
            jax.ShapeDtypeStruct((rows, width), F32),
            jax.ShapeDtypeStruct((rows, width), BF16),
            jax.ShapeDtypeStruct((packed // 2, LANES), F32),
            jax.ShapeDtypeStruct((packed // 2, LANES), BF16),
        ],
        scratch_shapes=[
            pltpu.VMEM((rows, width), BF16),
            pltpu.SemaphoreType.DMA,
            pltpu.VMEM((packed, LANES), F32),
            pltpu.VMEM((rows, width), BF16),
            pltpu.VMEM((rows, width), F32),
            pltpu.VMEM((rows, width), F32),
            pltpu.VMEM((rows, 1), F32),
            pltpu.VMEM((rows, width), F32),
            pltpu.VMEM((rows, width), BF16),
            pltpu.VMEM((rows, width), BF16),
            pltpu.VMEM((2, rows, 512), F32),
            pltpu.VMEM((2, rows, 512), BF16),
            pltpu.VMEM((rows, ff), BF16),
        ],
        compiler_params=params(23),
        cost_estimate=cost(
            8 * rows * width * (ff + width), 4 * width * ff + 12 * rows * width, rows * ff
        ),
        name="middle",
    )(me, x, og, ctx, out_weight, ffn_in, ffn_out, *small)


def back_begin(n, pair, base, refs, dp_ref):
    dc_ref, ct_ref, st_ref, e_ref, kv_ref, q_ref = refs
    head_dim = LANES // 2
    at = lanes(pair)
    d_ctx = dc_ref[:, at].T.astype(F32)
    outs = []
    weighted = []
    for which in range(2):
        span = slice(which * head_dim, (which + 1) * head_dim)
        part = (d_ctx[span] * st_ref[pair, base + which : base + which + 1]).astype(BF16)
        weighted.append(part)
        outs.append(rows_sum(part.astype(F32) * ct_ref[at][span]))
    do_t = jnp.concatenate(weighted, axis=0)
    for which in range(2):
        dp_ref[n, which] = mm(
            kv_ref[:, lanes(pair, q_ref.shape[1])], head_rows(do_t, which, head_dim)
        )
    return do_t.T, outs


def both_heads(left, right):
    half = LANES // 2
    return mm(
        jnp.concatenate(left, axis=1),
        jnp.concatenate([head_lanes(right, 0, half), head_lanes(right, 1, half)], axis=0),
    )


def back_scores(n, pair, outs, e_ref, dp_ref, ds_ref):
    rows = dp_ref.shape[2]
    for which in range(2):
        for r in range(0, rows, TILE):
            e = e_ref[2 * pair + which, r : r + TILE].astype(F32)
            d_scores = e * (dp_ref[n, which, r : r + TILE] - outs[which])
            ds_ref[n, which, r : r + TILE] = d_scores.astype(BF16)


def back_pairs(pairs, base, refs, dp_ref, ds_ref):
    e_ref, kv_ref, q_ref = refs[3:]
    head_dim = LANES // 2
    scale = 1.0 / math.sqrt(head_dim)
    begun = [back_begin(n, pair, base, refs, dp_ref) for n, pair in enumerate(pairs)]
    results = []
    for n, pair in enumerate(pairs):
        do, outs = begun[n]
        back_scores(n, pair, outs, e_ref, dp_ref, ds_ref)
        results.append(both_heads([e_ref[2 * pair], e_ref[2 * pair + 1]], do))
    for n, pair in enumerate(pairs):
        kt = kv_ref[:, lanes(pair)].T
        dq = [mm(kt[w * head_dim : (w + 1) * head_dim], ds_ref[n, w]) for w in range(2)]
        dk = both_heads([ds_ref[n, 0], ds_ref[n, 1]], q_ref[:, lanes(pair)])
        yield n, jnp.concatenate(dq, axis=0) * scale, dk * scale, results[n]


def back_far_kernel(pairs, *refs):
    ins, (dqt_ref, dkv_ref, dp_ref, ds_ref) = refs[:6], refs[6:]
    for n, dqt, dk, dv in back_pairs(pairs, 2, ins, dp_ref, ds_ref):
        dqt_ref[lanes(n)] = dqt
        dkv_ref[:, lanes(2 * n)] = dk.astype(BF16)
        dkv_ref[:, lanes(2 * n + 1)] = dv.astype(BF16)


def back_near_kernel(pairs, places, *refs):
    ins, (w_ref, begun_ref), refs = refs[:6], refs[6:8], refs[8:]
    shares, (out_ref, dp_ref, ds_ref, all_ref) = refs[:-4], refs[-4:]
    width = begun_ref.shape[1]
    count = len(pairs)
    for n, dqt, dk, dv in back_pairs(pairs, 0, ins, dp_ref, ds_ref):
        group, at = places[n]
        dqt_ref, came_ref = shares[2 * group : 2 * group + 2]
        all_ref[:, lanes(n)] = (dqt + dqt_ref[lanes(at)]).astype(BF16).T
        all_ref[:, lanes(count + n)] = (dk + came_ref[:, lanes(2 * at)].astype(F32)).astype(BF16)
        all_ref[:, lanes(2 * count + n)] = (
            dv + came_ref[:, lanes(2 * at + 1)].astype(F32)
        ).astype(BF16)
    columns = [lanes(pair, kind * width) for kind in range(3) for pair in pairs]
    weights = jnp.concatenate([w_ref[:, column] for column in columns], axis=1)
    out_ref[...] = (begun_ref[...] + mm(all_ref[...], weights, NT)).astype(out_ref.dtype)


def back_scratch(rows, count):
    return [
        pltpu.VMEM((count, 2, rows, rows), F32),
        pltpu.VMEM((count, 2, rows, rows), BF16),
    ]


def attend_back_far(pairs, d_ctx, ct, st, e, kv, q):
    rows, width = q.shape
    count = len(pairs)
    return pl.pallas_call(
        functools.partial(back_far_kernel, pairs),
        in_specs=[VMEM] * 6,
        out_specs=[VMEM] * 2,
        out_shape=[
            jax.ShapeDtypeStruct((count * LANES, rows), F32),
            jax.ShapeDtypeStruct((rows, 2 * count * LANES), BF16),
        ],
        scratch_shapes=back_scratch(rows, count),
        compiler_params=params(26),
        cost_estimate=cost(20 * rows * rows * LANES * count, 6 * rows * rows * count),
        name="back_far",
    )(d_ctx, ct, st, e, kv, q)


def attend_back_near(pairs, shares, dtype, d_ctx, ct, st, e, kv, q, weight, begun):
    rows, width = q.shape
    count = len(pairs)
    used = [group for group in shares if set(group) & set(pairs)]
    places = [
        next((i, group.index(pair)) for i, group in enumerate(used) if pair in group)
        for pair in pairs
    ]
    return pl.pallas_call(
        functools.partial(back_near_kernel, pairs, places),
        in_specs=[VMEM] * (8 + 2 * len(used)),
        out_specs=VMEM,
        out_shape=jax.ShapeDtypeStruct((rows, width), dtype),
        scratch_shapes=back_scratch(rows, count) + [pltpu.VMEM((rows, 3 * count * LANES), BF16)],
        compiler_params=params(28),
        cost_estimate=cost(30 * rows * rows * LANES * count, 6 * rows * rows * count),
        name="back_near",
    )(d_ctx, ct, st, e, kv, q, weight, begun, *(x for group in used for x in shares[group]))


def trade(value, devices, even, odd):
    moves = [(i, i ^ (odd if i % 2 else even)) for i in range(devices)]
    return lax.ppermute(value, ("dp", "seq"), moves)


def bit_order(devices):
    bits = [1 << i for i in range(1, (devices - 1).bit_length())]
    order = []
    for i in range(0, len(bits) - 1, 2):
        order += [(bits[i], bits[i + 1]), (bits[i + 1], bits[i])]
    return order + ([(bits[-1], bits[-1])] if len(bits) % 2 else [])


def sum_kernel(own_ref, came_ref, sum_ref):
    sum_ref[...] = (own_ref[...].astype(F32) + came_ref[...].astype(F32)).astype(BF16)


def add_pair(own, came):
    vmem = pl.BlockSpec(memory_space=pltpu.VMEM)
    return pl.pallas_call(
        sum_kernel,
        in_specs=[vmem] * 2,
        out_specs=vmem,
        out_shape=jax.ShapeDtypeStruct(own.shape, BF16),
        compiler_params=params(6),
        cost_estimate=cost(own.size, 8 * own.size),
        name="add_pair",
    )(own, came)


def unpack_kernel(me_ref, own_ref, came_ref, *refs):
    outs, all_ref = refs[:-1], refs[-1]
    half = own_ref.shape[0]
    side = lax.rem(me_ref[0], 2)
    for place, ref in ((side, own_ref), (1 - side, came_ref)):
        all_ref[pl.ds(pl.multiple_of(place * half, half), half), :] = ref[...].astype(F32)
    up2, down2, up1, down1, ub1, ub2, g1, b1, g2, b2, db1, db2, r1, r2 = outs
    adapt, width = up2.shape
    at = 0
    for ref in (up2, down2, up1, down1):
        for lo in range(0, width, LANES):
            ref[:, lo : lo + LANES] = all_ref[at : at + adapt]
            at += adapt
    for ref in (ub1, ub2, g1, b1, g2, b2):
        for lo in range(0, width, LANES):
            ref[lo : lo + LANES] = all_ref[at]
            at += 1
    biases = all_ref[at : at + 1]
    db1[...] = biases[:, :adapt]
    db2[...] = biases[:, adapt:]
    roots = jnp.sqrt(all_ref[at + 1 : at + 2])
    r1[...] = roots[:, 0:1] / roots[:, 1:2]
    r2[...] = roots[:, 2:3] / roots[:, 3:4]


def unpack(me, own, came, adapt, width):
    vmem = pl.BlockSpec(memory_space=pltpu.VMEM)
    shapes = [(adapt, width)] * 4 + [(width,)] * 6 + [(1, adapt)] * 2 + [(1, 1)] * 2
    return pl.pallas_call(
        unpack_kernel,
        in_specs=[pl.BlockSpec(memory_space=pltpu.SMEM), vmem, vmem],
        out_specs=[vmem] * len(shapes),
        out_shape=[jax.ShapeDtypeStruct(s, F32) for s in shapes],
        scratch_shapes=[pltpu.VMEM((2 * own.shape[0], LANES), F32)],
        compiler_params=params(6),
        cost_estimate=cost(4 * adapt * width, 24 * adapt * width),
        name="unpack",
    )(me, own, came)


def sum_stages(me, own, other, devices, adapt, width):
    came = trade(other, devices, 1, 1)
    beside = yield
    own = add_pair(own, after(beside, came))
    yield own
    for even, odd in bit_order(devices):
        came = trade(own, devices, even, odd)
        beside = yield
        own = add_pair(own, after(beside, came))
        yield own
    came = trade(own, devices, 1, 1)
    beside = yield
    yield unpack(me, own, after(beside, came), adapt, width)
    while True:
        yield None


def beside(stages, kernel_result, operand, sums):
    done = stages.send(kernel_result)
    if done is None:
        return operand, sums
    operand = after(done, operand)
    next(stages)
    return operand, done


def after(done, value):
    return lax.optimization_barrier((value, done))[0]


def per_device(
    hidden_in,
    out_grad,
    segments,
    qkv_weight,
    out_weight,
    ffn_in,
    ffn_out,
    first_down,
    first_down_bias,
    first_up,
    first_up_bias,
    second_down,
    second_down_bias,
    second_up,
    second_up_bias,
    norm1_gain,
    norm1_bias,
    norm2_gain,
    norm2_bias,
):
    seqs, half, width = hidden_in.shape
    adapt = first_down.shape[1]
    assert seqs == 1
    x = hidden_in.reshape(half, width)
    og = out_grad.reshape(half, width)
    devices = lax.axis_size("dp") * 2
    me = (lax.axis_index("dp") * 2 + lax.axis_index("seq")).astype(jnp.int32).reshape(1)
    swap = [(0, 1), (1, 0)]

    kv, q = project(x, qkv_weight)
    kv_came = lax.ppermute(kv, "seq", swap)
    near_ct, near_st, near_e = attend_near(me, q, kv, segments)
    kv_far, ctx, ct, st, far_e = attend_far(me, q, kv_came, segments, near_ct, near_st)
    layer_out, d_first, d_ctx, own, other = middle(
        x,
        og,
        ctx,
        out_weight,
        ffn_in,
        ffn_out,
        (
            first_down.T,
            first_down_bias,
            first_up,
            first_up_bias,
            second_down.T,
            second_down_bias,
            second_up,
            second_up_bias,
            norm1_gain,
            norm1_bias,
            norm2_gain,
            norm2_bias,
        ),
        me,
        packed_rows(adapt, width),
    )
    stages = sum_stages(me, own, other, devices, adapt, width)
    next(stages)
    plan = (
        ((False, (0, 1)),),
        ((False, (2, 3)),),
        ((False, (4,)),),
        ((False, (5,)), (True, (0, 1))),
        ((True, (2, 3, 4)),),
        ((True, (5,)),),
    )
    sums = None
    shares = {}
    begun = d_first
    for line in plan:
        for near, pairs in line:
            if near:
                dtype = BF16 if line is plan[-1] else F32
                begun = attend_back_near(
                    pairs, shares, dtype, d_ctx, ct, st, near_e, kv, q, qkv_weight, begun
                )
                result = begun
            else:
                result, dkv = attend_back_far(pairs, d_ctx, ct, st, far_e, kv_far, q)
                shares[pairs] = (result, lax.ppermute(dkv, "seq", swap))
        st, sums = beside(stages, result, st, sums)
    input_grad = begun
    for unused in range(2 + devices.bit_length()):
        st, sums = beside(stages, begun, st, sums)
    up2, down2, up1, down1, ub1, ub2, g1, b1, g2, b2, db1, db2, r1, r2 = sums
    return (
        layer_out.reshape(1, half, width),
        input_grad.reshape(1, half, width),
        down1.T,
        db1.reshape(adapt),
        up1,
        ub1,
        down2.T,
        db2.reshape(adapt),
        up2,
        ub2,
        g1,
        b1,
        g2,
        b2,
        r1.reshape(()),
        r2.reshape(()),
    )


def solution(mesh):
    split = P("dp", "seq", None)
    return jax.shard_map(
        per_device,
        mesh=mesh,
        in_specs=(split, split, P("dp", None)) + (P(),) * 16,
        out_specs=(split, split) + (P(),) * 14,
        check_vma=False,
    )
```

```python
import functools
import math

import jax
import jax.numpy as jnp
from jax import lax
from jax.experimental import pallas as pl
from jax.experimental.pallas import tpu as pltpu
from jax.sharding import PartitionSpec as P

HEADS = 12
F32 = jnp.float32
BF16 = jnp.bfloat16
LOG2E = math.log2(math.e)
MASKED = -1.0e9
MIB = 1024 * 1024
LANES = 128
TILE = 32

NN = (((1,), (0,)), ((), ()))
NT = (((1,), (1,)), ((), ()))
TN = (((0,), (0,)), ((), ()))


def mm(left, right, dims=NN):
    return lax.dot_general(left, right, dims, preferred_element_type=F32)


def gelu_pair(v):
    cdf = 0.5 + 0.5 * lax.erf(v * math.sqrt(0.5))
    bell = jnp.exp2(v * v * (-0.5 * LOG2E))
    return v * cdf, cdf + v * bell * (1.0 / math.sqrt(2.0 * math.pi))


def row(ref):
    return ref[...].reshape(1, -1)


def rows_sum(value):
    return jnp.sum(value, axis=0, keepdims=True)


def lanes_mean(value):
    return jnp.mean(value, axis=-1, keepdims=True)


def fold(value):
    return jnp.sum(value.reshape(-1, 8, value.shape[-1]), axis=0)


def each_tile(rows, tile, body, sums):
    for at in range(0, rows, tile):
        sums = body(slice(at, at + tile), sums)
    return sums


def total(value):
    return jnp.sum(rows_sum(value), axis=1, keepdims=True)


def norm_forward(resid):
    center = resid - lanes_mean(resid)
    rstd = lax.rsqrt(lanes_mean(center * center) + 1e-12)
    return center * rstd, rstd


def packed_rows(adapt, width):
    rows = 4 * adapt * (width // LANES) + 6 * (width // LANES) + 2
    return -(-rows // 64) * 64


def put_packed(ref, number, value):
    rows, width = value.shape
    for i in range(width // LANES):
        at = (number * (width // LANES) + i) * rows
        ref[at : at + rows] = value[:, i * LANES : (i + 1) * LANES]


def norm_backward(xhat, rstd, dxhat):
    return rstd * (dxhat - lanes_mean(dxhat) - xhat * lanes_mean(dxhat * xhat))


def head_lanes(pair, which, head_dim):
    lane = lax.broadcasted_iota(jnp.int32, pair.shape, 1)
    keep = (lane < head_dim) if which == 0 else (lane >= head_dim)
    return jnp.where(keep, pair, jnp.zeros_like(pair))


def head_rows(pair, which, head_dim):
    part = pair[which * head_dim : (which + 1) * head_dim]
    blank = jnp.zeros_like(part)
    return jnp.concatenate([part, blank] if which == 0 else [blank, part], axis=0)


def params(vmem=20, **more):
    return pltpu.CompilerParams(vmem_limit_bytes=vmem * MIB, **more)


def cost(flops, moved, exps=0):
    return pl.CostEstimate(flops=int(flops), bytes_accessed=int(moved), transcendentals=int(exps))


def stay(*arrays):
    return [pltpu.with_memory_space_constraint(x, pltpu.HBM) for x in arrays]


def qkv_kernel(x_hbm, w_hbm, kv_ref, q_ref, x_ref, w_ref, sem):
    width = x_ref.shape[1]
    load_x = pltpu.make_async_copy(x_hbm, x_ref, sem.at[3])
    load_x.start()
    loads = []
    for i, part in enumerate((1, 2, 0)):
        span = pl.ds(part * width, width)
        loads.append(pltpu.make_async_copy(w_hbm.at[:, span], w_ref.at[i], sem.at[i]))
        loads[-1].start()
    load_x.wait()
    for i in range(2):
        loads[i].wait()
        kv_ref[:, i * width : (i + 1) * width] = mm(x_ref[...], w_ref[i]).astype(BF16)
    loads[2].wait()
    q_ref[...] = mm(x_ref[...], w_ref[2]).astype(BF16)


VMEM = pl.BlockSpec(memory_space=pltpu.VMEM)
SMEM = pl.BlockSpec(memory_space=pltpu.SMEM)
HBM = pl.BlockSpec(memory_space=pl.ANY)


def project(x, qkv_weight):
    rows, width = x.shape
    return pl.pallas_call(
        qkv_kernel,
        in_specs=[HBM, HBM],
        out_specs=[VMEM] * 2,
        out_shape=[
            jax.ShapeDtypeStruct((rows, 2 * width), BF16),
            jax.ShapeDtypeStruct((rows, width), BF16),
        ],
        scratch_shapes=[
            pltpu.VMEM((rows, width), BF16),
            pltpu.VMEM((3, width, width), BF16),
            pltpu.SemaphoreType.DMA((4,)),
        ],
        compiler_params=params(16),
        cost_estimate=cost(6 * rows * width * width, 6 * width * width),
        name="project",
    )(*stay(x, qkv_weight))


def fill_bias(bias_ref, ids_ref, key_side, query_side):
    half = bias_ref.shape[0]
    keys = ids_ref[:, pl.ds(pl.multiple_of(key_side * half, half), half)].astype(F32)
    queries = ids_ref[:, pl.ds(pl.multiple_of(query_side * half, half), half)].astype(F32)
    column = jnp.broadcast_to(keys, (LANES, half)).T
    for lo in range(0, half, LANES):
        bias_ref[:, lo : lo + LANES] = jnp.where(column == queries[:, lo : lo + LANES], 0.0, MASKED)


def softmax_head(level_ref, bias_ref, unit, e_ref, floor=None):
    rows, columns = level_ref.shape
    peak = None
    for r in range(0, rows, TILE):
        level = level_ref[r : r + TILE] * unit + bias_ref[r : r + TILE]
        level_ref[r : r + TILE] = level
        part = jnp.max(level.reshape(-1, 8, columns), axis=0)
        peak = part if peak is None else jnp.maximum(peak, part)
    top = jnp.max(peak, axis=0, keepdims=True)
    if floor is not None:
        top = jnp.maximum(top, floor)
    mass = None
    for r in range(0, rows, TILE):
        e = jnp.exp2(level_ref[r : r + TILE] - top)
        e_ref[r : r + TILE] = e.astype(BF16)
        mass = fold(e) if mass is None else mass + fold(e)
    return top, rows_sum(mass)


def lanes(pair, base=0):
    return slice(base + pair * LANES, base + (pair + 1) * LANES)


def score_head(level_ref, q_ref, kv_ref, head):
    at = lanes(head // 2)
    queries = head_rows(q_ref[:, at].T, head % 2, LANES // 2)
    level_ref[...] = mm(kv_ref[:, at], queries)


def near_kernel(me_ref, q_ref, kv_ref, ids_ref, ct_ref, st_ref, e_ref, bias_ref, level_ref):
    side = lax.rem(me_ref[0], 2)
    fill_bias(bias_ref, ids_ref, side, side)
    width = q_ref.shape[1]
    head_dim = LANES // 2
    unit = LOG2E / math.sqrt(head_dim)
    score_head(level_ref.at[0], q_ref, kv_ref, 0)
    for head in range(HEADS):
        if head + 1 < HEADS:
            score_head(level_ref.at[(head + 1) % 2], q_ref, kv_ref, head + 1)
        pair, which = head // 2, head % 2
        top, mass = softmax_head(level_ref.at[head % 2], bias_ref, unit, e_ref.at[head])
        values = kv_ref[:, lanes(pair, width)].T[which * head_dim : (which + 1) * head_dim]
        ct_ref[head * head_dim : (head + 1) * head_dim] = mm(values, e_ref[head])
        st_ref[pair, which : which + 1] = top
        st_ref[pair, 2 + which : 3 + which] = mass


def attend_near(me, q, kv, ids):
    rows, width = q.shape
    pairs = width // LANES
    return pl.pallas_call(
        near_kernel,
        in_specs=[SMEM] + [VMEM] * 3,
        out_specs=[VMEM] * 3,
        out_shape=[
            jax.ShapeDtypeStruct((width, rows), F32),
            jax.ShapeDtypeStruct((pairs, 8, rows), F32),
            jax.ShapeDtypeStruct((HEADS, rows, rows), BF16),
        ],
        scratch_shapes=[pltpu.VMEM((rows, rows), F32), pltpu.VMEM((2, rows, rows), F32)],
        compiler_params=params(14),
        cost_estimate=cost(8 * rows * rows * width, 3 * HEADS * rows * rows, HEADS * rows * rows),
        name="attend_near",
    )(me, q, kv, ids)


def far_kernel(
    me_ref,
    q_ref,
    came_hbm,
    ids_ref,
    cn_ref,
    sn_ref,
    kv_ref,
    c_ref,
    ct_ref,
    st_ref,
    e_ref,
    bias_ref,
    level_ref,
    sem,
):
    width = q_ref.shape[1]
    loads = []
    for i in range(2):
        span = pl.ds(i * width, width)
        loads.append(pltpu.make_async_copy(came_hbm.at[:, span], kv_ref.at[:, span], sem.at[i]))
        loads[i].start()
    side = lax.rem(me_ref[0], 2)
    fill_bias(bias_ref, ids_ref, 1 - side, side)
    head_dim = LANES // 2
    unit = LOG2E / math.sqrt(head_dim)
    loads[0].wait()
    score_head(level_ref.at[0], q_ref, kv_ref, 0)
    loads[1].wait()
    for head in range(HEADS):
        if head + 1 < HEADS:
            score_head(level_ref.at[(head + 1) % 2], q_ref, kv_ref, head + 1)
        pair, which = head // 2, head % 2
        near_top = sn_ref[pair, which : which + 1]
        near_mass = sn_ref[pair, 2 + which : 3 + which]
        top, mass = softmax_head(level_ref.at[head % 2], bias_ref, unit, e_ref.at[head], near_top)
        near_part = jnp.exp2(near_top - top)
        inverse = 1.0 / (mass + near_mass * near_part)
        values = kv_ref[:, lanes(pair, width)].T[which * head_dim : (which + 1) * head_dim]
        rows = slice(head * head_dim, (head + 1) * head_dim)
        ct_ref[rows] = (mm(values, e_ref[head]) + cn_ref[rows] * near_part) * inverse
        st_ref[pair, which : which + 1] = near_part * inverse
        st_ref[pair, 2 + which : 3 + which] = inverse
        if which:
            c_ref[:, lanes(pair)] = ct_ref[lanes(pair)].astype(BF16).T


def attend_far(me, q, came, ids, near_ct, near_st):
    rows, width = q.shape
    pairs = width // LANES
    return pl.pallas_call(
        far_kernel,
        in_specs=[SMEM, VMEM, HBM] + [VMEM] * 3,
        out_specs=[VMEM] * 5,
        out_shape=[
            jax.ShapeDtypeStruct((rows, 2 * width), BF16),
            jax.ShapeDtypeStruct((rows, width), BF16),
            jax.ShapeDtypeStruct((width, rows), F32),
            jax.ShapeDtypeStruct((pairs, 8, rows), F32),
            jax.ShapeDtypeStruct((HEADS, rows, rows), BF16),
        ],
        scratch_shapes=[
            pltpu.VMEM((rows, rows), F32),
            pltpu.VMEM((2, rows, rows), F32),
            pltpu.SemaphoreType.DMA((2,)),
        ],
        compiler_params=params(14),
        cost_estimate=cost(6 * rows * rows * width, 3 * HEADS * rows * rows, HEADS * rows * rows),
        name="attend_far",
    )(me, q, came, ids, near_ct, near_st)


def middle_kernel(
    me_ref,
    x_ref,
    og_ref,
    c_ref,
    wo_ref,
    fi_hbm,
    fo_ref,
    d1_ref,
    bd1_ref,
    u1_ref,
    bu1_ref,
    d2_ref,
    bd2_ref,
    u2_ref,
    bu2_ref,
    g1_ref,
    b1_ref,
    g2_ref,
    b2_ref,
    out_hbm,
    df_ref,
    dc_ref,
    *rest,
):
    own_ref, other_ref, *scratch = rest
    (
        fi_ref,
        load_sem,
        out_ref,
        sem,
        grad_ref,
        attn_ref,
        branch_ref,
        xhat_ref,
        rstd_ref,
        normed_ref,
        nb_ref,
        post_ref,
        pre_ref,
        act_ref,
        slope_ref,
    ) = scratch
    db_ref, acc_ref = nb_ref, branch_ref
    load = pltpu.make_async_copy(fi_hbm, fi_ref, load_sem)
    load.start()

    rows, width = x_ref.shape
    ff = fi_ref.shape[1]
    wide = pre_ref.shape[2]
    chunks = ff // wide
    none = jnp.zeros((8, width), F32)

    attn_ref[...] = mm(c_ref[...], wo_ref[...]).astype(BF16)
    hidden, slope_one = gelu_pair(mm(attn_ref[...], d1_ref[...], NT) + row(bd1_ref))
    hidden_one = hidden.astype(BF16)
    branch_ref[...] = mm(hidden_one, u1_ref[...])

    def first_norm(at, sums):
        x = x_ref[at].astype(F32)
        branch = branch_ref[at] + row(bu1_ref)
        xhat, rstd = norm_forward(x + attn_ref[at].astype(F32) + branch)
        normed = xhat * row(g1_ref) + row(b1_ref)
        xhat_ref[at] = xhat
        rstd_ref[at] = rstd
        normed_ref[at] = normed
        nb_ref[at] = normed.astype(BF16)
        terms = (branch * branch, x * x, normed * normed)
        return tuple(a + fold(b) for a, b in zip(sums, terms))

    branch_sq, input_sq, normed_sq = map(total, each_tile(rows, 32, first_norm, (none,) * 3))

    load.wait()
    pre_ref[0] = mm(nb_ref[...], fi_ref[:, :wide])
    for j in range(chunks):
        if j + 1 < chunks:
            pre_ref[(j + 1) % 2] = mm(nb_ref[...], fi_ref[:, (j + 1) * wide : (j + 2) * wide])
        for r in range(0, rows, 16):
            act, slope = gelu_pair(pre_ref[j % 2, r : r + 16])
            act_ref[j % 2, r : r + 16] = act.astype(BF16)
            slope_ref[r : r + 16, j * wide : (j + 1) * wide] = slope.astype(BF16)
        part = mm(act_ref[j % 2], fo_ref[j * wide : (j + 1) * wide])
        if j == 0:
            acc_ref[...] = part
        else:
            acc_ref[...] += part

    post_ref[...] = acc_ref[...].astype(BF16)
    hidden, slope_two = gelu_pair(mm(post_ref[...], d2_ref[...], NT) + row(bd2_ref))
    hidden_two = hidden.astype(BF16)
    branch_ref[...] = mm(hidden_two, u2_ref[...])

    def second_norm(at, sums):
        branch = branch_ref[at] + row(bu2_ref)
        xhat, rstd = norm_forward(normed_ref[at] + post_ref[at].astype(F32) + branch)
        out_ref[at] = (xhat * row(g2_ref) + row(b2_ref)).astype(BF16)
        og = og_ref[at].astype(F32)
        d_second = norm_backward(xhat, rstd, og * row(g2_ref))
        d_branch = d_second.astype(BF16)
        normed_ref[at] = d_second
        db_ref[at] = d_branch
        terms = (branch * branch, og * xhat, og, d_branch.astype(F32))
        return tuple(a + fold(b) for a, b in zip(sums, terms))

    second_sq, gain2, bias2, up_bias2 = each_tile(rows, 32, second_norm, (none,) * 4)
    save = pltpu.make_async_copy(out_ref, out_hbm, sem)
    save.start()
    second_sq = total(second_sq)
    gain2, bias2, up_bias2 = map(rows_sum, (gain2, bias2, up_bias2))
    put_packed(grad_ref, 0, mm(hidden_two, db_ref[...], TN))
    d_pre = (mm(db_ref[...], u2_ref[...], NT) * slope_two).astype(BF16)
    put_packed(grad_ref, 1, mm(d_pre, post_ref[...], TN))
    down_bias2 = rows_sum(d_pre.astype(F32))
    post_ref[...] = (normed_ref[...] + mm(d_pre, d2_ref[...])).astype(BF16)

    pre_ref[0] = mm(post_ref[...], fo_ref[:wide], NT)
    for j in range(chunks):
        if j + 1 < chunks:
            pre_ref[(j + 1) % 2] = mm(post_ref[...], fo_ref[(j + 1) * wide : (j + 2) * wide], NT)
        for r in range(0, rows, 16):
            slope = slope_ref[r : r + 16, j * wide : (j + 1) * wide].astype(F32)
            act_ref[j % 2, r : r + 16] = (pre_ref[j % 2, r : r + 16] * slope).astype(BF16)
        part = mm(act_ref[j % 2], fi_ref[:, j * wide : (j + 1) * wide], NT)
        if j == 0:
            acc_ref[...] = part
        else:
            acc_ref[...] += part

    def first_back(at, sums):
        d_normed = normed_ref[at] + acc_ref[at]
        xhat = xhat_ref[at]
        d_first = norm_backward(xhat, rstd_ref[at], d_normed * row(g1_ref))
        d_branch = d_first.astype(BF16)
        df_ref[at] = d_first
        db_ref[at] = d_branch
        terms = (d_normed * xhat, d_normed, d_branch.astype(F32))
        return tuple(a + fold(b) for a, b in zip(sums, terms))

    gain1, bias1, up_bias1 = map(rows_sum, each_tile(rows, 32, first_back, (none,) * 3))
    put_packed(grad_ref, 2, mm(hidden_one, db_ref[...], TN))
    d_pre = (mm(db_ref[...], u1_ref[...], NT) * slope_one).astype(BF16)
    put_packed(grad_ref, 3, mm(d_pre, attn_ref[...], TN))
    down_bias1 = rows_sum(d_pre.astype(F32))
    d_attn = (df_ref[...] + mm(d_pre, d1_ref[...])).astype(BF16)
    dc_ref[...] = mm(d_attn, wo_ref[...], NT).astype(BF16)

    lane = lax.broadcasted_iota(jnp.int32, (1, LANES), 1)
    sums = jnp.where(lane == 0, branch_sq, 0.0)
    sums = jnp.where(lane == 1, input_sq, sums)
    sums = jnp.where(lane == 2, second_sq, sums)
    sums = jnp.where(lane == 3, normed_sq, sums)
    at = 4 * d1_ref.shape[0] * (width // LANES)
    grad_ref[at:] = jnp.zeros((grad_ref.shape[0] - at, LANES), F32)
    for vector in (up_bias1, up_bias2, gain1, bias1, gain2, bias2):
        for lo in range(0, width, LANES):
            grad_ref[at : at + 1] = vector[:, lo : lo + LANES]
            at += 1
    grad_ref[at : at + 1] = jnp.concatenate([down_bias1, down_bias2], axis=1)
    grad_ref[at + 1 : at + 2] = sums
    save.wait()
    half = grad_ref.shape[0] // 2
    side = lax.rem(me_ref[0], 2)
    own_ref[...] = grad_ref[pl.ds(pl.multiple_of(side * half, half), half), :]
    other_ref[...] = grad_ref[pl.ds(pl.multiple_of((1 - side) * half, half), half), :].astype(BF16)


def middle(x, og, ctx, out_weight, ffn_in, ffn_out, small, me, packed):
    rows, width = x.shape
    ff = ffn_in.shape[1]
    adapt = small[0].shape[0]
    vmem = pl.BlockSpec(memory_space=pltpu.VMEM)
    smem = pl.BlockSpec(memory_space=pltpu.SMEM)
    return pl.pallas_call(
        middle_kernel,
        in_specs=[smem] + [vmem] * 4 + [HBM] + [vmem] * (1 + len(small)),
        out_specs=[HBM] + [vmem] * 4,
        out_shape=[
            pltpu.HBM((rows, width), BF16),
            jax.ShapeDtypeStruct((rows, width), F32),
            jax.ShapeDtypeStruct((rows, width), BF16),
            jax.ShapeDtypeStruct((packed // 2, LANES), F32),
            jax.ShapeDtypeStruct((packed // 2, LANES), BF16),
        ],
        scratch_shapes=[
            pltpu.VMEM((width, ff), BF16),
            pltpu.SemaphoreType.DMA,
            pltpu.VMEM((rows, width), BF16),
            pltpu.SemaphoreType.DMA,
            pltpu.VMEM((packed, LANES), F32),
            pltpu.VMEM((rows, width), BF16),
            pltpu.VMEM((rows, width), F32),
            pltpu.VMEM((rows, width), F32),
            pltpu.VMEM((rows, 1), F32),
            pltpu.VMEM((rows, width), F32),
            pltpu.VMEM((rows, width), BF16),
            pltpu.VMEM((rows, width), BF16),
            pltpu.VMEM((2, rows, 512), F32),
            pltpu.VMEM((2, rows, 512), BF16),
            pltpu.VMEM((rows, ff), BF16),
        ],
        compiler_params=params(28),
        cost_estimate=cost(
            8 * rows * width * (ff + width), 4 * width * ff + 12 * rows * width, rows * ff
        ),
        name="middle",
    )(me, x, og, ctx, out_weight, *stay(ffn_in), ffn_out, *small)


def back_begin(n, pair, base, refs, dp_ref):
    dc_ref, ct_ref, st_ref, e_ref, kv_ref, q_ref = refs
    head_dim = LANES // 2
    at = lanes(pair)
    d_ctx = dc_ref[:, at].T.astype(F32)
    outs = []
    weighted = []
    for which in range(2):
        span = slice(which * head_dim, (which + 1) * head_dim)
        part = (d_ctx[span] * st_ref[pair, base + which : base + which + 1]).astype(BF16)
        weighted.append(part)
        outs.append(rows_sum(part.astype(F32) * ct_ref[at][span]))
    do_t = jnp.concatenate(weighted, axis=0)
    for which in range(2):
        dp_ref[n, which] = mm(
            kv_ref[:, lanes(pair, q_ref.shape[1])], head_rows(do_t, which, head_dim)
        )
    return do_t.T, outs


def both_heads(left, right):
    half = LANES // 2
    return mm(
        jnp.concatenate(left, axis=1),
        jnp.concatenate([head_lanes(right, 0, half), head_lanes(right, 1, half)], axis=0),
    )


def back_scores(n, pair, outs, e_ref, dp_ref, ds_ref):
    rows = dp_ref.shape[2]
    for which in range(2):
        for r in range(0, rows, TILE):
            e = e_ref[2 * pair + which, r : r + TILE].astype(F32)
            d_scores = e * (dp_ref[n, which, r : r + TILE] - outs[which])
            ds_ref[n, which, r : r + TILE] = d_scores.astype(BF16)


def back_pairs(pairs, base, refs, dp_ref, ds_ref):
    e_ref, kv_ref, q_ref = refs[3:]
    head_dim = LANES // 2
    scale = 1.0 / math.sqrt(head_dim)
    begun = [back_begin(n, pair, base, refs, dp_ref) for n, pair in enumerate(pairs)]
    results = []
    for n, pair in enumerate(pairs):
        do, outs = begun[n]
        back_scores(n, pair, outs, e_ref, dp_ref, ds_ref)
        results.append(both_heads([e_ref[2 * pair], e_ref[2 * pair + 1]], do))
    for n, pair in enumerate(pairs):
        kt = kv_ref[:, lanes(pair)].T
        dq = [mm(kt[w * head_dim : (w + 1) * head_dim], ds_ref[n, w]) for w in range(2)]
        dk = both_heads([ds_ref[n, 0], ds_ref[n, 1]], q_ref[:, lanes(pair)])
        yield n, jnp.concatenate(dq, axis=0) * scale, dk * scale, results[n]


def back_far_kernel(pairs, *refs):
    ins, (dqt_ref, dkv_ref, dp_ref, ds_ref) = refs[:6], refs[6:]
    for n, dqt, dk, dv in back_pairs(pairs, 2, ins, dp_ref, ds_ref):
        dqt_ref[lanes(n)] = dqt
        dkv_ref[:, lanes(2 * n)] = dk.astype(BF16)
        dkv_ref[:, lanes(2 * n + 1)] = dv.astype(BF16)


def back_near_kernel(pairs, places, *refs):
    ins, (w_ref, begun_ref), refs = refs[:6], refs[6:8], refs[8:]
    shares, (out_ref, dp_ref, ds_ref, all_ref) = refs[:-4], refs[-4:]
    width = begun_ref.shape[1]
    count = len(pairs)
    for n, dqt, dk, dv in back_pairs(pairs, 0, ins, dp_ref, ds_ref):
        group, at = places[n]
        dqt_ref, came_ref = shares[2 * group : 2 * group + 2]
        all_ref[:, lanes(n)] = (dqt + dqt_ref[lanes(at)]).astype(BF16).T
        all_ref[:, lanes(count + n)] = (dk + came_ref[:, lanes(2 * at)].astype(F32)).astype(BF16)
        all_ref[:, lanes(2 * count + n)] = (
            dv + came_ref[:, lanes(2 * at + 1)].astype(F32)
        ).astype(BF16)
    columns = [lanes(pair, kind * width) for kind in range(3) for pair in pairs]
    weights = jnp.concatenate([w_ref[:, column] for column in columns], axis=1)
    out_ref[...] = (begun_ref[...] + mm(all_ref[...], weights, NT)).astype(out_ref.dtype)


def back_scratch(rows, count):
    return [
        pltpu.VMEM((count, 2, rows, rows), F32),
        pltpu.VMEM((count, 2, rows, rows), BF16),
    ]


def attend_back_far(pairs, d_ctx, ct, st, e, kv, q):
    rows, width = q.shape
    count = len(pairs)
    return pl.pallas_call(
        functools.partial(back_far_kernel, pairs),
        in_specs=[VMEM] * 6,
        out_specs=[VMEM] * 2,
        out_shape=[
            jax.ShapeDtypeStruct((count * LANES, rows), F32),
            jax.ShapeDtypeStruct((rows, 2 * count * LANES), BF16),
        ],
        scratch_shapes=back_scratch(rows, count),
        compiler_params=params(26),
        cost_estimate=cost(60 * rows * rows * LANES * count, 6 * rows * rows * count),
        name="back_far",
    )(d_ctx, ct, st, e, kv, q)


def attend_back_near(pairs, shares, dtype, d_ctx, ct, st, e, kv, q, weight, begun):
    rows, width = q.shape
    count = len(pairs)
    used = [group for group in shares if set(group) & set(pairs)]
    places = [
        next((i, group.index(pair)) for i, group in enumerate(used) if pair in group)
        for pair in pairs
    ]
    return pl.pallas_call(
        functools.partial(back_near_kernel, pairs, places),
        in_specs=[VMEM] * (8 + 2 * len(used)),
        out_specs=VMEM,
        out_shape=jax.ShapeDtypeStruct((rows, width), dtype),
        scratch_shapes=back_scratch(rows, count) + [pltpu.VMEM((rows, 3 * count * LANES), BF16)],
        compiler_params=params(28),
        cost_estimate=cost(90 * rows * rows * LANES * count, 6 * rows * rows * count),
        name="back_near",
    )(d_ctx, ct, st, e, kv, q, weight, begun, *(x for group in used for x in shares[group]))


def trade(value, devices, bits):
    even, odd = bits
    moves = [(i, i ^ (odd if i % 2 else even)) for i in range(devices)]
    return lax.ppermute(value, ("dp", "seq"), moves)


def bit_order(devices):
    bits = [1 << i for i in range(1, (devices - 1).bit_length())]
    order = []
    for i in range(0, len(bits) - 1, 2):
        order += [(bits[i], bits[i + 1]), (bits[i + 1], bits[i])]
    return order + ([(bits[-1], bits[-1])] if len(bits) % 2 else [])


def add_kernel(own_ref, came_ref, sum_ref):
    sum_ref[...] = (own_ref[...].astype(F32) + came_ref[...].astype(F32)).astype(BF16)


def call_small(kernel, name, operands, shapes, scratch=()):
    specs = [VMEM if x.ndim > 1 else SMEM for x in operands]
    return pl.pallas_call(
        kernel,
        in_specs=specs,
        out_specs=[VMEM] * len(shapes),
        out_shape=shapes,
        scratch_shapes=list(scratch),
        compiler_params=params(6),
        cost_estimate=cost(operands[-1].size, 8 * operands[-1].size),
        name=name,
    )(*operands)


def add_pair(own, came):
    return call_small(add_kernel, "add_pair", (own, came), [jax.ShapeDtypeStruct(own.shape, BF16)])[0]


def bit_of(me_ref, bits):
    even, odd = bits
    number = me_ref[0]
    bit = jnp.where(lax.rem(number, 2) == 0, even, odd)
    return lax.rem(lax.div(number, bit), 2)


def split_kernel(bits, me_ref, own_ref, came_ref, keep_ref, send_ref, sum_ref):
    sum_ref[...] = own_ref[...] + came_ref[...].astype(F32)
    size = keep_ref.shape[0]
    place = bit_of(me_ref, bits)
    for at, ref in ((place, keep_ref), (1 - place, send_ref)):
        ref[...] = sum_ref[pl.ds(pl.multiple_of(at * size, size), size), :].astype(BF16)


def add_split(me, own, came, bits):
    rows, columns = own.shape
    return call_small(
        functools.partial(split_kernel, bits),
        "add_split",
        (me, own, came),
        [jax.ShapeDtypeStruct((rows // 2, columns), BF16)] * 2,
        [pltpu.VMEM((rows, columns), F32)],
    )


def join_kernel(bits, me_ref, own_ref, came_ref, all_ref, wide_ref):
    size = own_ref.shape[0]
    place = bit_of(me_ref, bits)
    for at, ref in ((place, own_ref), (1 - place, came_ref)):
        wide_ref[pl.ds(pl.multiple_of(at * size, size), size), :] = ref[...].astype(F32)
    all_ref[...] = wide_ref[...].astype(BF16)


def join(me, own, came, bits):
    rows, columns = own.shape
    return call_small(
        functools.partial(join_kernel, bits),
        "join",
        (me, own, came),
        [jax.ShapeDtypeStruct((2 * rows, columns), BF16)],
        [pltpu.VMEM((2 * rows, columns), F32)],
    )[0]


def unpack_kernel(me_ref, own_ref, came_ref, *refs):
    outs, all_ref = refs[:-1], refs[-1]
    half = own_ref.shape[0]
    side = lax.rem(me_ref[0], 2)
    for place, ref in ((side, own_ref), (1 - side, came_ref)):
        all_ref[pl.ds(pl.multiple_of(place * half, half), half), :] = ref[...].astype(F32)
    up2, down2, up1, down1, ub1, ub2, g1, b1, g2, b2, db1, db2, r1, r2 = outs
    adapt, width = up2.shape
    at = 0
    for ref in (up2, down2, up1, down1):
        for lo in range(0, width, LANES):
            ref[:, lo : lo + LANES] = all_ref[at : at + adapt]
            at += adapt
    for ref in (ub1, ub2, g1, b1, g2, b2):
        for lo in range(0, width, LANES):
            ref[lo : lo + LANES] = all_ref[at]
            at += 1
    biases = all_ref[at : at + 1]
    db1[...] = biases[:, :adapt]
    db2[...] = biases[:, adapt:]
    roots = jnp.sqrt(all_ref[at + 1 : at + 2])
    r1[...] = roots[:, 0:1] / roots[:, 1:2]
    r2[...] = roots[:, 2:3] / roots[:, 3:4]


def unpack(me, own, came, adapt, width):
    vmem = pl.BlockSpec(memory_space=pltpu.VMEM)
    shapes = [(adapt, width)] * 4 + [(width,)] * 6 + [(1, adapt)] * 2 + [(1, 1)] * 2
    return pl.pallas_call(
        unpack_kernel,
        in_specs=[pl.BlockSpec(memory_space=pltpu.SMEM), vmem, vmem],
        out_specs=[vmem] * len(shapes),
        out_shape=[jax.ShapeDtypeStruct(s, F32) for s in shapes],
        scratch_shapes=[pltpu.VMEM((2 * own.shape[0], LANES), F32)],
        compiler_params=params(6),
        cost_estimate=cost(4 * adapt * width, 24 * adapt * width),
        name="unpack",
    )(me, own, came)


def sum_stages(me, own, other, devices, adapt, width):
    came = trade(other, devices, (1, 1))
    beside = yield
    order = bit_order(devices)
    if order:
        own, send = add_split(me, own, after(beside, came), order[0])
        yield own
        came = trade(send, devices, order[0])
        beside = yield
    own = add_pair(own, after(beside, came))
    yield own
    for bits in order[1:]:
        came = trade(own, devices, bits)
        beside = yield
        own = add_pair(own, after(beside, came))
        yield own
    if order:
        came = trade(own, devices, order[0])
        beside = yield
        own = join(me, own, after(beside, came), order[0])
        yield own
    came = trade(own, devices, (1, 1))
    beside = yield
    yield unpack(me, own, after(beside, came), adapt, width)
    while True:
        yield None


def beside(stages, kernel_result, operand, sums):
    done = stages.send(kernel_result)
    if done is None:
        return operand, sums
    operand = after(done, operand)
    next(stages)
    return operand, done


def after(done, value):
    return lax.optimization_barrier((value, done))[0]


def per_device(
    hidden_in,
    out_grad,
    segments,
    qkv_weight,
    out_weight,
    ffn_in,
    ffn_out,
    first_down,
    first_down_bias,
    first_up,
    first_up_bias,
    second_down,
    second_down_bias,
    second_up,
    second_up_bias,
    norm1_gain,
    norm1_bias,
    norm2_gain,
    norm2_bias,
):
    seqs, half, width = hidden_in.shape
    adapt = first_down.shape[1]
    assert seqs == 1
    x = hidden_in.reshape(half, width)
    og = out_grad.reshape(half, width)
    devices = lax.axis_size("dp") * 2
    me = (lax.axis_index("dp") * 2 + lax.axis_index("seq")).astype(jnp.int32).reshape(1)
    swap = [(0, 1), (1, 0)]

    kv, q = project(x, qkv_weight)
    kv_came = lax.ppermute(kv, "seq", swap)
    near_ct, near_st, near_e = attend_near(me, q, kv, segments)
    kv_far, ctx, ct, st, far_e = attend_far(me, q, kv_came, segments, near_ct, near_st)
    layer_out, d_first, d_ctx, own, other = middle(
        x,
        og,
        ctx,
        out_weight,
        ffn_in,
        ffn_out,
        (
            first_down.T,
            first_down_bias,
            first_up,
            first_up_bias,
            second_down.T,
            second_down_bias,
            second_up,
            second_up_bias,
            norm1_gain,
            norm1_bias,
            norm2_gain,
            norm2_bias,
        ),
        me,
        packed_rows(adapt, width),
    )
    stages = sum_stages(me, own, other, devices, adapt, width)
    next(stages)
    plan = (
        ((False, (0,)),),
        ((False, (1, 2)),),
        ((False, (3, 4)),),
        ((False, (5,)), (True, (0,)),),
        ((True, (1, 2)),),
        ((True, (3, 4)),),
        ((True, (5,)),),
    )
    sums = None
    shares = {}
    begun = d_first
    for line in plan:
        for near, pairs in line:
            if near:
                dtype = BF16 if line is plan[-1] else F32
                begun = attend_back_near(
                    pairs, shares, dtype, d_ctx, ct, st, near_e, kv, q, qkv_weight, begun
                )
                result = begun
            else:
                result, dkv = attend_back_far(pairs, d_ctx, ct, st, far_e, kv_far, q)
                shares[pairs] = (result, lax.ppermute(dkv, "seq", swap))
        st, sums = beside(stages, result, st, sums)
    input_grad = begun
    for unused in range(2 + devices.bit_length()):
        st, sums = beside(stages, begun, st, sums)
    up2, down2, up1, down1, ub1, ub2, g1, b1, g2, b2, db1, db2, r1, r2 = sums
    return (
        layer_out.reshape(1, half, width),
        input_grad.reshape(1, half, width),
        down1.T,
        db1.reshape(adapt),
        up1,
        ub1,
        down2.T,
        db2.reshape(adapt),
        up2,
        ub2,
        g1,
        b1,
        g2,
        b2,
        r1.reshape(()),
        r2.reshape(()),
    )


def solution(mesh):
    split = P("dp", "seq", None)
    return jax.shard_map(
        per_device,
        mesh=mesh,
        in_specs=(split, split, P("dp", None)) + (P(),) * 16,
        out_specs=(split, split) + (P(),) * 14,
        check_vma=False,
    )
```

```python
import functools
import math

import jax
import jax.numpy as jnp
from jax import lax
from jax.experimental import pallas as pl
from jax.experimental.pallas import tpu as pltpu
from jax.sharding import PartitionSpec as P

HEADS = 12
F32 = jnp.float32
BF16 = jnp.bfloat16
LOG2E = math.log2(math.e)
MASKED = -1.0e9
MIB = 1024 * 1024
LANES = 128
TILE = 32

NN = (((1,), (0,)), ((), ()))
NT = (((1,), (1,)), ((), ()))
TN = (((0,), (0,)), ((), ()))


def mm(left, right, dims=NN):
    return lax.dot_general(left, right, dims, preferred_element_type=F32)


def gelu_pair(v):
    cdf = 0.5 + 0.5 * lax.erf(v * math.sqrt(0.5))
    bell = jnp.exp2(v * v * (-0.5 * LOG2E))
    return v * cdf, cdf + v * bell * (1.0 / math.sqrt(2.0 * math.pi))


def row(ref):
    return ref[...].reshape(1, -1)


def rows_sum(value):
    return jnp.sum(value, axis=0, keepdims=True)


def lanes_mean(value):
    return jnp.mean(value, axis=-1, keepdims=True)


def fold(value):
    return jnp.sum(value.reshape(-1, 8, value.shape[-1]), axis=0)


def each_tile(rows, tile, body, sums):
    for at in range(0, rows, tile):
        sums = body(slice(at, at + tile), sums)
    return sums


def total(value):
    return jnp.sum(rows_sum(value), axis=1, keepdims=True)


def norm_forward(resid):
    center = resid - lanes_mean(resid)
    rstd = lax.rsqrt(lanes_mean(center * center) + 1e-12)
    return center * rstd, rstd


def packed_rows(adapt, width):
    rows = 4 * adapt * (width // LANES) + 6 * (width // LANES) + 2
    return -(-rows // 128) * 128


def put_packed(ref, number, value):
    rows, width = value.shape
    for i in range(width // LANES):
        at = (number * (width // LANES) + i) * rows
        ref[at : at + rows] = value[:, i * LANES : (i + 1) * LANES]


def norm_backward(xhat, rstd, dxhat):
    return rstd * (dxhat - lanes_mean(dxhat) - xhat * lanes_mean(dxhat * xhat))


def head_lanes(pair, which, head_dim):
    lane = lax.broadcasted_iota(jnp.int32, pair.shape, 1)
    keep = (lane < head_dim) if which == 0 else (lane >= head_dim)
    return jnp.where(keep, pair, jnp.zeros_like(pair))


def head_rows(pair, which, head_dim):
    part = pair[which * head_dim : (which + 1) * head_dim]
    blank = jnp.zeros_like(part)
    return jnp.concatenate([part, blank] if which == 0 else [blank, part], axis=0)


def params(vmem=20, **more):
    return pltpu.CompilerParams(vmem_limit_bytes=vmem * MIB, **more)


def cost(flops, moved, exps=0):
    return pl.CostEstimate(flops=int(flops), bytes_accessed=int(moved), transcendentals=int(exps))


def stay(*arrays):
    return [pltpu.with_memory_space_constraint(x, pltpu.HBM) for x in arrays]


def qkv_kernel(x_hbm, w_hbm, k_ref, v_ref, q_ref, x_ref, w_ref, sem):
    width = x_ref.shape[1]
    load_x = pltpu.make_async_copy(x_hbm, x_ref, sem.at[3])
    load_x.start()
    loads = []
    for i, part in enumerate((1, 2, 0)):
        span = pl.ds(part * width, width)
        loads.append(pltpu.make_async_copy(w_hbm.at[:, span], w_ref.at[i], sem.at[i]))
        loads[-1].start()
    load_x.wait()
    for i, out_ref in enumerate((k_ref, v_ref, q_ref)):
        loads[i].wait()
        out_ref[...] = mm(x_ref[...], w_ref[i]).astype(BF16)


VMEM = pl.BlockSpec(memory_space=pltpu.VMEM)
SMEM = pl.BlockSpec(memory_space=pltpu.SMEM)
HBM = pl.BlockSpec(memory_space=pl.ANY)


def project(x, qkv_weight):
    rows, width = x.shape
    return pl.pallas_call(
        qkv_kernel,
        in_specs=[HBM, HBM],
        out_specs=[VMEM] * 3,
        out_shape=[jax.ShapeDtypeStruct((rows, width), BF16)] * 3,
        scratch_shapes=[
            pltpu.VMEM((rows, width), BF16),
            pltpu.VMEM((3, width, width), BF16),
            pltpu.SemaphoreType.DMA((4,)),
        ],
        compiler_params=params(9),
        cost_estimate=cost(6 * rows * width * width, 6 * width * width),
        name="project",
    )(*stay(x, qkv_weight))


def fill_bias(bias_ref, ids_ref, key_side, query_side):
    half = bias_ref.shape[0]
    keys = ids_ref[:, pl.ds(pl.multiple_of(key_side * half, half), half)].astype(F32)
    queries = ids_ref[:, pl.ds(pl.multiple_of(query_side * half, half), half)].astype(F32)
    column = jnp.broadcast_to(keys, (LANES, half)).T
    for lo in range(0, half, LANES):
        bias_ref[:, lo : lo + LANES] = jnp.where(column == queries[:, lo : lo + LANES], 0.0, MASKED)


def softmax_head(level_ref, bias_ref, unit, e_ref, floor=None):
    rows, columns = level_ref.shape
    peak = None
    for r in range(0, rows, TILE):
        level = level_ref[r : r + TILE] * unit + bias_ref[r : r + TILE]
        level_ref[r : r + TILE] = level
        part = jnp.max(level.reshape(-1, 8, columns), axis=0)
        peak = part if peak is None else jnp.maximum(peak, part)
    top = jnp.max(peak, axis=0, keepdims=True)
    if floor is not None:
        top = jnp.maximum(top, floor)
    mass = None
    for r in range(0, rows, TILE):
        e = jnp.exp2(level_ref[r : r + TILE] - top)
        e_ref[r : r + TILE] = e.astype(BF16)
        mass = fold(e) if mass is None else mass + fold(e)
    return top, rows_sum(mass)


def lanes(pair, base=0):
    return slice(base + pair * LANES, base + (pair + 1) * LANES)


def score_head(level_ref, q_ref, k_ref, head):
    at = lanes(head // 2)
    queries = head_rows(q_ref[:, at].T, head % 2, LANES // 2)
    level_ref[...] = mm(k_ref[:, at], queries)


def near_kernel(me_ref, q_ref, k_ref, v_ref, ids_ref, ct_ref, st_ref, e_ref, bias_ref, level_ref):
    side = lax.rem(me_ref[0], 2)
    fill_bias(bias_ref, ids_ref, side, side)
    width = q_ref.shape[1]
    head_dim = LANES // 2
    unit = LOG2E / math.sqrt(head_dim)
    score_head(level_ref.at[0], q_ref, k_ref, 0)
    for head in range(HEADS):
        if head + 1 < HEADS:
            score_head(level_ref.at[(head + 1) % 2], q_ref, k_ref, head + 1)
        pair, which = head // 2, head % 2
        top, mass = softmax_head(level_ref.at[head % 2], bias_ref, unit, e_ref.at[head])
        values = v_ref[:, lanes(pair)].T[which * head_dim : (which + 1) * head_dim]
        ct_ref[head * head_dim : (head + 1) * head_dim] = mm(values, e_ref[head])
        st_ref[pair, which : which + 1] = top
        st_ref[pair, 2 + which : 3 + which] = mass


def attend_near(me, q, k, v, ids):
    rows, width = q.shape
    pairs = width // LANES
    return pl.pallas_call(
        near_kernel,
        in_specs=[SMEM] + [VMEM] * 4,
        out_specs=[VMEM] * 3,
        out_shape=[
            jax.ShapeDtypeStruct((width, rows), F32),
            jax.ShapeDtypeStruct((pairs, 8, rows), F32),
            jax.ShapeDtypeStruct((HEADS, rows, rows), BF16),
        ],
        scratch_shapes=[pltpu.VMEM((rows, rows), F32), pltpu.VMEM((2, rows, rows), F32)],
        compiler_params=params(6),
        cost_estimate=cost(8 * rows * rows * width, 3 * HEADS * rows * rows, HEADS * rows * rows),
        name="attend_near",
    )(me, q, k, v, ids)


def far_kernel(
    me_ref,
    q_ref,
    k_hbm,
    v_hbm,
    ids_ref,
    cn_ref,
    sn_ref,
    k_ref,
    v_ref,
    c_ref,
    ct_ref,
    st_ref,
    e_ref,
    bias_ref,
    level_ref,
    sem,
):
    loads = []
    for i, (came, ref) in enumerate(((k_hbm, k_ref), (v_hbm, v_ref))):
        loads.append(pltpu.make_async_copy(came, ref, sem.at[i]))
        loads[i].start()
    side = lax.rem(me_ref[0], 2)
    fill_bias(bias_ref, ids_ref, 1 - side, side)
    head_dim = LANES // 2
    unit = LOG2E / math.sqrt(head_dim)
    loads[0].wait()
    score_head(level_ref.at[0], q_ref, k_ref, 0)
    loads[1].wait()
    for head in range(HEADS):
        if head + 1 < HEADS:
            score_head(level_ref.at[(head + 1) % 2], q_ref, k_ref, head + 1)
        pair, which = head // 2, head % 2
        near_top = sn_ref[pair, which : which + 1]
        near_mass = sn_ref[pair, 2 + which : 3 + which]
        top, mass = softmax_head(level_ref.at[head % 2], bias_ref, unit, e_ref.at[head], near_top)
        near_part = jnp.exp2(near_top - top)
        inverse = 1.0 / (mass + near_mass * near_part)
        values = v_ref[:, lanes(pair)].T[which * head_dim : (which + 1) * head_dim]
        rows = slice(head * head_dim, (head + 1) * head_dim)
        ct_ref[rows] = (mm(values, e_ref[head]) + cn_ref[rows] * near_part) * inverse
        st_ref[pair, which : which + 1] = near_part * inverse
        st_ref[pair, 2 + which : 3 + which] = inverse
        if which:
            c_ref[:, lanes(pair)] = ct_ref[lanes(pair)].astype(BF16).T


def attend_far(me, q, k, v, ids, near_ct, near_st):
    rows, width = q.shape
    pairs = width // LANES
    return pl.pallas_call(
        far_kernel,
        in_specs=[SMEM, VMEM, HBM, HBM] + [VMEM] * 3,
        out_specs=[VMEM] * 6,
        out_shape=[
            jax.ShapeDtypeStruct((rows, width), BF16),
            jax.ShapeDtypeStruct((rows, width), BF16),
            jax.ShapeDtypeStruct((rows, width), BF16),
            jax.ShapeDtypeStruct((width, rows), F32),
            jax.ShapeDtypeStruct((pairs, 8, rows), F32),
            jax.ShapeDtypeStruct((HEADS, rows, rows), BF16),
        ],
        scratch_shapes=[
            pltpu.VMEM((rows, rows), F32),
            pltpu.VMEM((2, rows, rows), F32),
            pltpu.SemaphoreType.DMA((2,)),
        ],
        compiler_params=params(6),
        cost_estimate=cost(6 * rows * rows * width, 3 * HEADS * rows * rows, HEADS * rows * rows),
        name="attend_far",
    )(me, q, k, v, ids, near_ct, near_st)


def middle_kernel(
    me_ref,
    x_ref,
    og_ref,
    c_ref,
    wo_ref,
    fi_ref,
    fo_ref,
    d1_ref,
    bd1_ref,
    u1_ref,
    bu1_ref,
    d2_ref,
    bd2_ref,
    u2_ref,
    bu2_ref,
    g1_ref,
    b1_ref,
    g2_ref,
    b2_ref,
    out_hbm,
    df_ref,
    dc_ref,
    *rest,
):
    own_ref, other_ref, *scratch = rest
    (
        out_ref,
        sem,
        grad_ref,
        attn_ref,
        branch_ref,
        xhat_ref,
        rstd_ref,
        normed_ref,
        nb_ref,
        post_ref,
        pre_ref,
        act_ref,
        slope_ref,
    ) = scratch
    db_ref, acc_ref = nb_ref, branch_ref

    rows, width = x_ref.shape
    ff = fi_ref.shape[1]
    wide = pre_ref.shape[2]
    chunks = ff // wide
    none = jnp.zeros((8, width), F32)

    attn_ref[...] = mm(c_ref[...], wo_ref[...]).astype(BF16)
    hidden, slope_one = gelu_pair(mm(attn_ref[...], d1_ref[...], NT) + row(bd1_ref))
    hidden_one = hidden.astype(BF16)
    branch_ref[...] = mm(hidden_one, u1_ref[...])

    def first_norm(at, sums):
        x = x_ref[at].astype(F32)
        branch = branch_ref[at] + row(bu1_ref)
        xhat, rstd = norm_forward(x + attn_ref[at].astype(F32) + branch)
        normed = xhat * row(g1_ref) + row(b1_ref)
        xhat_ref[at] = xhat
        rstd_ref[at] = rstd
        normed_ref[at] = normed
        nb_ref[at] = normed.astype(BF16)
        terms = (branch * branch, x * x, normed * normed)
        return tuple(a + fold(b) for a, b in zip(sums, terms))

    branch_sq, input_sq, normed_sq = map(total, each_tile(rows, 32, first_norm, (none,) * 3))

    pre_ref[0] = mm(nb_ref[...], fi_ref[:, :wide])
    for j in range(chunks):
        if j + 1 < chunks:
            pre_ref[(j + 1) % 2] = mm(nb_ref[...], fi_ref[:, (j + 1) * wide : (j + 2) * wide])
        for r in range(0, rows, 16):
            act, slope = gelu_pair(pre_ref[j % 2, r : r + 16])
            act_ref[j % 2, r : r + 16] = act.astype(BF16)
            slope_ref[r : r + 16, j * wide : (j + 1) * wide] = slope.astype(BF16)
        part = mm(act_ref[j % 2], fo_ref[j * wide : (j + 1) * wide])
        if j == 0:
            acc_ref[...] = part
        else:
            acc_ref[...] += part

    post_ref[...] = acc_ref[...].astype(BF16)
    hidden, slope_two = gelu_pair(mm(post_ref[...], d2_ref[...], NT) + row(bd2_ref))
    hidden_two = hidden.astype(BF16)
    branch_ref[...] = mm(hidden_two, u2_ref[...])

    def second_norm(at, sums):
        branch = branch_ref[at] + row(bu2_ref)
        xhat, rstd = norm_forward(normed_ref[at] + post_ref[at].astype(F32) + branch)
        out_ref[at] = (xhat * row(g2_ref) + row(b2_ref)).astype(BF16)
        og = og_ref[at].astype(F32)
        d_second = norm_backward(xhat, rstd, og * row(g2_ref))
        d_branch = d_second.astype(BF16)
        normed_ref[at] = d_second
        db_ref[at] = d_branch
        terms = (branch * branch, og * xhat, og, d_branch.astype(F32))
        return tuple(a + fold(b) for a, b in zip(sums, terms))

    second_sq, gain2, bias2, up_bias2 = each_tile(rows, 32, second_norm, (none,) * 4)
    save = pltpu.make_async_copy(out_ref, out_hbm, sem)
    save.start()
    second_sq = total(second_sq)
    gain2, bias2, up_bias2 = map(rows_sum, (gain2, bias2, up_bias2))
    put_packed(grad_ref, 0, mm(hidden_two, db_ref[...], TN))
    d_pre = (mm(db_ref[...], u2_ref[...], NT) * slope_two).astype(BF16)
    put_packed(grad_ref, 1, mm(d_pre, post_ref[...], TN))
    down_bias2 = rows_sum(d_pre.astype(F32))
    post_ref[...] = (normed_ref[...] + mm(d_pre, d2_ref[...])).astype(BF16)

    pre_ref[0] = mm(post_ref[...], fo_ref[:wide], NT)
    for j in range(chunks):
        if j + 1 < chunks:
            pre_ref[(j + 1) % 2] = mm(post_ref[...], fo_ref[(j + 1) * wide : (j + 2) * wide], NT)
        for r in range(0, rows, 16):
            slope = slope_ref[r : r + 16, j * wide : (j + 1) * wide].astype(F32)
            act_ref[j % 2, r : r + 16] = (pre_ref[j % 2, r : r + 16] * slope).astype(BF16)
        part = mm(act_ref[j % 2], fi_ref[:, j * wide : (j + 1) * wide], NT)
        if j == 0:
            acc_ref[...] = part
        else:
            acc_ref[...] += part

    def first_back(at, sums):
        d_normed = normed_ref[at] + acc_ref[at]
        xhat = xhat_ref[at]
        d_first = norm_backward(xhat, rstd_ref[at], d_normed * row(g1_ref))
        d_branch = d_first.astype(BF16)
        df_ref[at] = d_first
        db_ref[at] = d_branch
        terms = (d_normed * xhat, d_normed, d_branch.astype(F32))
        return tuple(a + fold(b) for a, b in zip(sums, terms))

    gain1, bias1, up_bias1 = map(rows_sum, each_tile(rows, 32, first_back, (none,) * 3))
    put_packed(grad_ref, 2, mm(hidden_one, db_ref[...], TN))
    d_pre = (mm(db_ref[...], u1_ref[...], NT) * slope_one).astype(BF16)
    put_packed(grad_ref, 3, mm(d_pre, attn_ref[...], TN))
    down_bias1 = rows_sum(d_pre.astype(F32))
    d_attn = (df_ref[...] + mm(d_pre, d1_ref[...])).astype(BF16)
    dc_ref[...] = mm(d_attn, wo_ref[...], NT).astype(BF16)

    lane = lax.broadcasted_iota(jnp.int32, (1, LANES), 1)
    sums = jnp.where(lane == 0, branch_sq, 0.0)
    sums = jnp.where(lane == 1, input_sq, sums)
    sums = jnp.where(lane == 2, second_sq, sums)
    sums = jnp.where(lane == 3, normed_sq, sums)
    at = 4 * d1_ref.shape[0] * (width // LANES)
    grad_ref[at:] = jnp.zeros((grad_ref.shape[0] - at, LANES), F32)
    for vector in (up_bias1, up_bias2, gain1, bias1, gain2, bias2):
        for lo in range(0, width, LANES):
            grad_ref[at : at + 1] = vector[:, lo : lo + LANES]
            at += 1
    grad_ref[at : at + 1] = jnp.concatenate([down_bias1, down_bias2], axis=1)
    grad_ref[at + 1 : at + 2] = sums
    save.wait()
    half = grad_ref.shape[0] // 2
    side = lax.rem(me_ref[0], 2)
    own_ref[...] = grad_ref[pl.ds(pl.multiple_of(side * half, half), half), :]
    other_ref[...] = grad_ref[pl.ds(pl.multiple_of((1 - side) * half, half), half), :].astype(BF16)


def middle(x, og, ctx, out_weight, ffn_in, ffn_out, small, me, packed):
    rows, width = x.shape
    ff = ffn_in.shape[1]
    adapt = small[0].shape[0]
    vmem = pl.BlockSpec(memory_space=pltpu.VMEM)
    smem = pl.BlockSpec(memory_space=pltpu.SMEM)
    return pl.pallas_call(
        middle_kernel,
        in_specs=[smem] + [vmem] * (6 + len(small)),
        out_specs=[HBM] + [vmem] * 4,
        out_shape=[
            pltpu.HBM((rows, width), BF16),
            jax.ShapeDtypeStruct((rows, width), F32),
            jax.ShapeDtypeStruct((rows, width), BF16),
            jax.ShapeDtypeStruct((packed // 2, LANES), F32),
            jax.ShapeDtypeStruct((packed // 2, LANES), BF16),
        ],
        scratch_shapes=[
            pltpu.VMEM((rows, width), BF16),
            pltpu.SemaphoreType.DMA,
            pltpu.VMEM((packed, LANES), F32),
            pltpu.VMEM((rows, width), BF16),
            pltpu.VMEM((rows, width), F32),
            pltpu.VMEM((rows, width), F32),
            pltpu.VMEM((rows, 1), F32),
            pltpu.VMEM((rows, width), F32),
            pltpu.VMEM((rows, width), BF16),
            pltpu.VMEM((rows, width), BF16),
            pltpu.VMEM((2, rows, 512), F32),
            pltpu.VMEM((2, rows, 512), BF16),
            pltpu.VMEM((rows, ff), BF16),
        ],
        compiler_params=params(19),
        cost_estimate=cost(
            8 * rows * width * (ff + width), 4 * width * ff + 12 * rows * width, rows * ff
        ),
        name="middle",
    )(me, x, og, ctx, out_weight, ffn_in, ffn_out, *small)


def back_begin(n, pair, base, refs, dp_ref):
    dc_ref, ct_ref, st_ref, e_ref, k_ref, v_ref, q_ref = refs
    head_dim = LANES // 2
    at = lanes(pair)
    d_ctx = dc_ref[:, at].T.astype(F32)
    outs = []
    weighted = []
    for which in range(2):
        span = slice(which * head_dim, (which + 1) * head_dim)
        part = (d_ctx[span] * st_ref[pair, base + which : base + which + 1]).astype(BF16)
        weighted.append(part)
        outs.append(rows_sum(part.astype(F32) * ct_ref[at][span]))
    do_t = jnp.concatenate(weighted, axis=0)
    for which in range(2):
        dp_ref[n, which] = mm(v_ref[:, at], head_rows(do_t, which, head_dim))
    return do_t.T, outs


def both_heads(left, right):
    half = LANES // 2
    return mm(
        jnp.concatenate(left, axis=1),
        jnp.concatenate([head_lanes(right, 0, half), head_lanes(right, 1, half)], axis=0),
    )


def back_scores(n, pair, outs, e_ref, dp_ref, ds_ref):
    rows = dp_ref.shape[2]
    for which in range(2):
        for r in range(0, rows, TILE):
            e = e_ref[2 * pair + which, r : r + TILE].astype(F32)
            d_scores = e * (dp_ref[n, which, r : r + TILE] - outs[which])
            ds_ref[n, which, r : r + TILE] = d_scores.astype(BF16)


def back_pairs(pairs, base, refs, dp_ref, ds_ref):
    e_ref, k_ref, v_ref, q_ref = refs[3:]
    head_dim = LANES // 2
    scale = 1.0 / math.sqrt(head_dim)
    begun = [back_begin(n, pair, base, refs, dp_ref) for n, pair in enumerate(pairs)]
    results = []
    for n, pair in enumerate(pairs):
        do, outs = begun[n]
        back_scores(n, pair, outs, e_ref, dp_ref, ds_ref)
        results.append(both_heads([e_ref[2 * pair], e_ref[2 * pair + 1]], do))
    for n, pair in enumerate(pairs):
        kt = k_ref[:, lanes(pair)].T
        dq = [mm(kt[w * head_dim : (w + 1) * head_dim], ds_ref[n, w]) for w in range(2)]
        dk = both_heads([ds_ref[n, 0], ds_ref[n, 1]], q_ref[:, lanes(pair)])
        yield n, jnp.concatenate(dq, axis=0) * scale, dk * scale, results[n]


def back_far_kernel(pairs, *refs):
    ins, (dqt_ref, dkv_ref, dp_ref, ds_ref) = refs[:7], refs[7:]
    for n, dqt, dk, dv in back_pairs(pairs, 2, ins, dp_ref, ds_ref):
        dqt_ref[lanes(n)] = dqt
        dkv_ref[:, lanes(2 * n)] = dk.astype(BF16)
        dkv_ref[:, lanes(2 * n + 1)] = dv.astype(BF16)


def back_near_kernel(pairs, places, *refs):
    ins, (w_ref, begun_ref), refs = refs[:7], refs[7:9], refs[9:]
    shares, (out_ref, dp_ref, ds_ref, all_ref) = refs[:-4], refs[-4:]
    width = begun_ref.shape[1]
    count = len(pairs)
    for n, dqt, dk, dv in back_pairs(pairs, 0, ins, dp_ref, ds_ref):
        group, at = places[n]
        dqt_ref, came_ref = shares[2 * group : 2 * group + 2]
        all_ref[:, lanes(n)] = (dqt + dqt_ref[lanes(at)]).astype(BF16).T
        all_ref[:, lanes(count + n)] = (dk + came_ref[:, lanes(2 * at)].astype(F32)).astype(BF16)
        all_ref[:, lanes(2 * count + n)] = (
            dv + came_ref[:, lanes(2 * at + 1)].astype(F32)
        ).astype(BF16)
    columns = [lanes(pair, kind * width) for kind in range(3) for pair in pairs]
    weights = jnp.concatenate([w_ref[:, column] for column in columns], axis=1)
    out_ref[...] = (begun_ref[...] + mm(all_ref[...], weights, NT)).astype(out_ref.dtype)


def back_scratch(rows, count):
    return [
        pltpu.VMEM((count, 2, rows, rows), F32),
        pltpu.VMEM((count, 2, rows, rows), BF16),
    ]


def attend_back_far(pairs, d_ctx, ct, st, e, k, v, q):
    rows, width = q.shape
    count = len(pairs)
    return pl.pallas_call(
        functools.partial(back_far_kernel, pairs),
        in_specs=[VMEM] * 7,
        out_specs=[VMEM] * 2,
        out_shape=[
            jax.ShapeDtypeStruct((count * LANES, rows), F32),
            jax.ShapeDtypeStruct((rows, 2 * count * LANES), BF16),
        ],
        scratch_shapes=back_scratch(rows, count),
        compiler_params=params(15),
        cost_estimate=cost(200 * rows * rows * LANES * count, 6 * rows * rows * count),
        name="back_far",
    )(d_ctx, ct, st, e, k, v, q)


def attend_back_near(pairs, shares, dtype, d_ctx, ct, st, e, k, v, q, weight, begun):
    rows, width = q.shape
    count = len(pairs)
    used = [group for group in shares if set(group) & set(pairs)]
    places = [
        next((i, group.index(pair)) for i, group in enumerate(used) if pair in group)
        for pair in pairs
    ]
    return pl.pallas_call(
        functools.partial(back_near_kernel, pairs, places),
        in_specs=[VMEM] * (9 + 2 * len(used)),
        out_specs=VMEM,
        out_shape=jax.ShapeDtypeStruct((rows, width), dtype),
        scratch_shapes=back_scratch(rows, count) + [pltpu.VMEM((rows, 3 * count * LANES), BF16)],
        compiler_params=params(16),
        cost_estimate=cost(300 * rows * rows * LANES * count, 6 * rows * rows * count),
        name="back_near",
    )(d_ctx, ct, st, e, k, v, q, weight, begun, *(x for group in used for x in shares[group]))


def levels_of(devices):
    levels = []
    stride = 2
    while stride < devices:
        size = math.gcd(devices // stride, 4)
        levels.append((stride, size))
        stride *= size
    return levels


def trade(values, devices, level):
    stride, size = level
    came = []
    for s in range(1, size):
        moves = []
        for i in range(devices):
            pos = i // stride % size
            moves.append((i, i + ((pos + s) % size - pos) * stride))
        came.append(lax.ppermute(values[s - 1], ("dp", "seq"), moves))
    return came


def call_small(kernel, name, operands, shapes, scratch=()):
    specs = [VMEM if x.ndim > 1 else SMEM for x in operands]
    return pl.pallas_call(
        kernel,
        in_specs=specs,
        out_specs=[VMEM] * len(shapes),
        out_shape=shapes,
        scratch_shapes=list(scratch),
        compiler_params=params(6),
        cost_estimate=cost(operands[-1].size, 8 * operands[-1].size),
        name=name,
    )(*operands)


def place_of(me_ref, level):
    stride, size = level
    return lax.rem(lax.div(me_ref[0], stride), size)


def split_kernel(level, me_ref, own_ref, came_ref, *refs):
    outs, sum_ref = refs[:-1], refs[-1]
    sum_ref[...] = own_ref[...].astype(F32) + came_ref[...].astype(F32)
    rows = outs[0].shape[0]
    place = place_of(me_ref, level)
    for s, ref in enumerate(outs):
        at = lax.rem(place + s, level[1]) * rows
        ref[...] = sum_ref[pl.ds(pl.multiple_of(at, rows), rows), :].astype(BF16)


def add_split(me, own, came, level):
    rows, columns = own.shape
    return call_small(
        functools.partial(split_kernel, level),
        "add_split",
        (me, own, came),
        [jax.ShapeDtypeStruct((rows // level[1], columns), BF16)] * level[1],
        [pltpu.VMEM((rows, columns), F32)],
    )


def add_kernel(level, me_ref, *refs):
    ins, out_ref, all_ref = refs[:-2], refs[-2], refs[-1]
    place = place_of(me_ref, level)
    for s, ref in enumerate(ins):
        all_ref[lax.rem(place + level[1] - s, level[1])] = ref[...].astype(F32)
    value = all_ref[0]
    for s in range(1, len(ins)):
        value = value + all_ref[s]
    out_ref[...] = value.astype(BF16)


def add_group(me, values, level):
    shape = values[0].shape
    return call_small(
        functools.partial(add_kernel, level),
        "add_group",
        (me, *values),
        [jax.ShapeDtypeStruct(shape, BF16)],
        [pltpu.VMEM((level[1], *shape), F32)],
    )[0]


def join_kernel(level, me_ref, *refs):
    ins, out_ref, all_ref = refs[:-2], refs[-2], refs[-1]
    rows = ins[0].shape[0]
    place = place_of(me_ref, level)
    for s, ref in enumerate(ins):
        at = lax.rem(place + level[1] - s, level[1]) * rows
        all_ref[pl.ds(pl.multiple_of(at, rows), rows), :] = ref[...].astype(F32)
    out_ref[...] = all_ref[...].astype(BF16)


def join(me, values, level):
    rows, columns = values[0].shape
    rows = rows * level[1]
    return call_small(
        functools.partial(join_kernel, level),
        "join",
        (me, *values),
        [jax.ShapeDtypeStruct((rows, columns), BF16)],
        [pltpu.VMEM((rows, columns), F32)],
    )[0]


def unpack_kernel(me_ref, own_ref, came_ref, *refs):
    outs, all_ref = refs[:-1], refs[-1]
    half = own_ref.shape[0]
    side = lax.rem(me_ref[0], 2)
    for place, ref in ((side, own_ref), (1 - side, came_ref)):
        all_ref[pl.ds(pl.multiple_of(place * half, half), half), :] = ref[...].astype(F32)
    up2, down2, up1, down1, ub1, ub2, g1, b1, g2, b2, db1, db2, r1, r2 = outs
    adapt, width = up2.shape
    at = 0
    for ref in (up2, down2, up1, down1):
        for lo in range(0, width, LANES):
            ref[:, lo : lo + LANES] = all_ref[at : at + adapt]
            at += adapt
    for ref in (ub1, ub2, g1, b1, g2, b2):
        for lo in range(0, width, LANES):
            ref[lo : lo + LANES] = all_ref[at]
            at += 1
    biases = all_ref[at : at + 1]
    db1[...] = biases[:, :adapt]
    db2[...] = biases[:, adapt:]
    roots = jnp.sqrt(all_ref[at + 1 : at + 2])
    r1[...] = roots[:, 0:1] / roots[:, 1:2]
    r2[...] = roots[:, 2:3] / roots[:, 3:4]


def unpack(me, own, came, adapt, width):
    vmem = pl.BlockSpec(memory_space=pltpu.VMEM)
    shapes = [(adapt, width)] * 4 + [(width,)] * 6 + [(1, adapt)] * 2 + [(1, 1)] * 2
    return pl.pallas_call(
        unpack_kernel,
        in_specs=[pl.BlockSpec(memory_space=pltpu.SMEM), vmem, vmem],
        out_specs=[vmem] * len(shapes),
        out_shape=[jax.ShapeDtypeStruct(s, F32) for s in shapes],
        scratch_shapes=[pltpu.VMEM((2 * own.shape[0], LANES), F32)],
        compiler_params=params(6),
        cost_estimate=cost(4 * adapt * width, 24 * adapt * width),
        name="unpack",
    )(me, own, came)


def sum_stages(me, own, other, devices, adapt, width):
    cores = (1, 2)
    levels = levels_of(devices) or [(2, 1)]
    (came,) = trade([other], devices, cores)
    beside = yield
    parts = add_split(me, own, after(beside, came), levels[0])
    yield parts[0]
    came = trade(parts[1:], devices, levels[0])
    beside = yield
    own = add_group(me, [parts[0], *after(beside, came)], levels[0])
    yield own
    for level in levels[1:]:
        came = trade([own] * level[1], devices, level)
        beside = yield
        own = add_group(me, [own, *after(beside, came)], level)
        yield own
    came = trade([own] * levels[0][1], devices, levels[0])
    beside = yield
    own = join(me, [own, *after(beside, came)], levels[0])
    yield own
    (came,) = trade([own], devices, cores)
    beside = yield
    yield unpack(me, own, after(beside, came), adapt, width)
    while True:
        yield None


def beside(stages, kernel_result, operand, sums):
    done = stages.send(kernel_result)
    if done is None:
        return operand, sums
    operand = after(done, operand)
    next(stages)
    return operand, done


def after(done, value):
    return lax.optimization_barrier((value, done))[0]


def per_device(
    hidden_in,
    out_grad,
    segments,
    qkv_weight,
    out_weight,
    ffn_in,
    ffn_out,
    first_down,
    first_down_bias,
    first_up,
    first_up_bias,
    second_down,
    second_down_bias,
    second_up,
    second_up_bias,
    norm1_gain,
    norm1_bias,
    norm2_gain,
    norm2_bias,
):
    seqs, half, width = hidden_in.shape
    adapt = first_down.shape[1]
    assert seqs == 1
    x = hidden_in.reshape(half, width)
    og = out_grad.reshape(half, width)
    devices = lax.axis_size("dp") * 2
    me = (lax.axis_index("dp") * 2 + lax.axis_index("seq")).astype(jnp.int32).reshape(1)
    swap = [(0, 1), (1, 0)]

    k, v, q = project(x, qkv_weight)
    k_came = lax.ppermute(k, "seq", swap)
    v_came = lax.ppermute(v, "seq", swap)
    near_ct, near_st, near_e = attend_near(me, q, k, v, segments)
    k_far, v_far, ctx, ct, st, far_e = attend_far(
        me, q, k_came, v_came, segments, near_ct, near_st
    )
    layer_out, d_first, d_ctx, own, other = middle(
        x,
        og,
        ctx,
        out_weight,
        ffn_in,
        ffn_out,
        (
            first_down.T,
            first_down_bias,
            first_up,
            first_up_bias,
            second_down.T,
            second_down_bias,
            second_up,
            second_up_bias,
            norm1_gain,
            norm1_bias,
            norm2_gain,
            norm2_bias,
        ),
        me,
        packed_rows(adapt, width),
    )
    stages = sum_stages(me, own, other, devices, adapt, width)
    next(stages)
    plan = (
        ((False, (0,)),),
        ((False, (1, 2, 3)),),
        ((False, (4, 5)), (True, (0, 1)),),
        ((True, (2, 3, 4)),),
        ((True, (5,)),),
    )
    sums = None
    shares = {}
    begun = d_first
    for line in plan:
        for near, pairs in line:
            if near:
                dtype = BF16 if line is plan[-1] else F32
                begun = attend_back_near(
                    pairs, shares, dtype, d_ctx, ct, st, near_e, k, v, q, qkv_weight, begun
                )
                result = begun
            else:
                result, dkv = attend_back_far(pairs, d_ctx, ct, st, far_e, k_far, v_far, q)
                shares[pairs] = (result, lax.ppermute(dkv, "seq", swap))
        st, sums = beside(stages, result, st, sums)
    input_grad = begun
    for unused in range(2 + devices.bit_length()):
        st, sums = beside(stages, begun, st, sums)
    up2, down2, up1, down1, ub1, ub2, g1, b1, g2, b2, db1, db2, r1, r2 = sums
    return (
        layer_out.reshape(1, half, width),
        input_grad.reshape(1, half, width),
        down1.T,
        db1.reshape(adapt),
        up1,
        ub1,
        down2.T,
        db2.reshape(adapt),
        up2,
        ub2,
        g1,
        b1,
        g2,
        b2,
        r1.reshape(()),
        r2.reshape(()),
    )


def solution(mesh):
    split = P("dp", "seq", None)
    return jax.shard_map(
        per_device,
        mesh=mesh,
        in_specs=(split, split, P("dp", None)) + (P(),) * 16,
        out_specs=(split, split) + (P(),) * 14,
        check_vma=False,
    )
```

```python
import functools
import math

import jax
import jax.numpy as jnp
from jax import lax
from jax.experimental import pallas as pl
from jax.experimental.pallas import tpu as pltpu
from jax.sharding import PartitionSpec as P

HEADS = 12
F32 = jnp.float32
BF16 = jnp.bfloat16
LOG2E = math.log2(math.e)
MASKED = -1.0e9
MIB = 1024 * 1024
LANES = 128
TILE = 32

NN = (((1,), (0,)), ((), ()))
NT = (((1,), (1,)), ((), ()))
TN = (((0,), (0,)), ((), ()))


def mm(left, right, dims=NN):
    return lax.dot_general(left, right, dims, preferred_element_type=F32)


def gelu_pair(v):
    cdf = 0.5 + 0.5 * lax.erf(v * math.sqrt(0.5))
    bell = jnp.exp2(v * v * (-0.5 * LOG2E))
    return v * cdf, cdf + v * bell * (1.0 / math.sqrt(2.0 * math.pi))


def row(ref):
    return ref[...].reshape(1, -1)


def rows_sum(value):
    return jnp.sum(value, axis=0, keepdims=True)


def lanes_mean(value):
    return jnp.mean(value, axis=-1, keepdims=True)


def fold(value):
    return jnp.sum(value.reshape(-1, 8, value.shape[-1]), axis=0)


def each_tile(rows, tile, body, sums):
    for at in range(0, rows, tile):
        sums = body(slice(at, at + tile), sums)
    return sums


def total(value):
    return jnp.sum(rows_sum(value), axis=1, keepdims=True)


def norm_forward(resid):
    center = resid - lanes_mean(resid)
    rstd = lax.rsqrt(lanes_mean(center * center) + 1e-12)
    return center * rstd, rstd


def packed_rows(adapt, width):
    rows = 4 * adapt * (width // LANES) + 6 * (width // LANES) + 2
    return -(-rows // 128) * 128


def put_packed(ref, number, value):
    rows, width = value.shape
    for i in range(width // LANES):
        at = (number * (width // LANES) + i) * rows
        ref[at : at + rows] = value[:, i * LANES : (i + 1) * LANES]


def norm_backward(xhat, rstd, dxhat):
    return rstd * (dxhat - lanes_mean(dxhat) - xhat * lanes_mean(dxhat * xhat))


def head_lanes(pair, which, head_dim):
    lane = lax.broadcasted_iota(jnp.int32, pair.shape, 1)
    keep = (lane < head_dim) if which == 0 else (lane >= head_dim)
    return jnp.where(keep, pair, jnp.zeros_like(pair))


def head_rows(pair, which, head_dim):
    part = pair[which * head_dim : (which + 1) * head_dim]
    blank = jnp.zeros_like(part)
    return jnp.concatenate([part, blank] if which == 0 else [blank, part], axis=0)


def params(vmem=20, **more):
    return pltpu.CompilerParams(vmem_limit_bytes=vmem * MIB, **more)


def cost(flops, moved, exps=0):
    return pl.CostEstimate(flops=int(flops), bytes_accessed=int(moved), transcendentals=int(exps))


def stay(*arrays):
    return [pltpu.with_memory_space_constraint(x, pltpu.HBM) for x in arrays]


def qkv_kernel(x_hbm, w_hbm, kv_ref, q_ref, x_ref, w_ref, sem):
    width = x_ref.shape[1]
    load_x = pltpu.make_async_copy(x_hbm, x_ref, sem.at[3])
    load_x.start()
    loads = []
    for i, part in enumerate((1, 2, 0)):
        span = pl.ds(part * width, width)
        loads.append(pltpu.make_async_copy(w_hbm.at[:, span], w_ref.at[i], sem.at[i]))
        loads[-1].start()
    load_x.wait()
    for i in range(2):
        loads[i].wait()
        kv_ref[:, i * width : (i + 1) * width] = mm(x_ref[...], w_ref[i]).astype(BF16)
    loads[2].wait()
    q_ref[...] = mm(x_ref[...], w_ref[2]).astype(BF16)


VMEM = pl.BlockSpec(memory_space=pltpu.VMEM)
SMEM = pl.BlockSpec(memory_space=pltpu.SMEM)
HBM = pl.BlockSpec(memory_space=pl.ANY)


def project(x, qkv_weight):
    rows, width = x.shape
    return pl.pallas_call(
        qkv_kernel,
        in_specs=[HBM, HBM],
        out_specs=[VMEM] * 2,
        out_shape=[
            jax.ShapeDtypeStruct((rows, 2 * width), BF16),
            jax.ShapeDtypeStruct((rows, width), BF16),
        ],
        scratch_shapes=[
            pltpu.VMEM((rows, width), BF16),
            pltpu.VMEM((3, width, width), BF16),
            pltpu.SemaphoreType.DMA((4,)),
        ],
        compiler_params=params(9),
        cost_estimate=cost(6 * rows * width * width, 6 * width * width),
        name="project",
    )(*stay(x, qkv_weight))


def fill_bias(bias_ref, ids_ref, key_side, query_side):
    half = bias_ref.shape[0]
    keys = ids_ref[:, pl.ds(pl.multiple_of(key_side * half, half), half)].astype(F32)
    queries = ids_ref[:, pl.ds(pl.multiple_of(query_side * half, half), half)].astype(F32)
    column = jnp.broadcast_to(keys, (LANES, half)).T
    for lo in range(0, half, LANES):
        bias_ref[:, lo : lo + LANES] = jnp.where(column == queries[:, lo : lo + LANES], 0.0, MASKED)


def softmax_head(level_ref, bias_ref, unit, e_ref, floor=None):
    rows, columns = level_ref.shape
    peak = None
    for r in range(0, rows, TILE):
        level = level_ref[r : r + TILE] * unit + bias_ref[r : r + TILE]
        level_ref[r : r + TILE] = level
        part = jnp.max(level.reshape(-1, 8, columns), axis=0)
        peak = part if peak is None else jnp.maximum(peak, part)
    top = jnp.max(peak, axis=0, keepdims=True)
    if floor is not None:
        top = jnp.maximum(top, floor)
    mass = None
    for r in range(0, rows, TILE):
        e = jnp.exp2(level_ref[r : r + TILE] - top)
        e_ref[r : r + TILE] = e.astype(BF16)
        mass = fold(e) if mass is None else mass + fold(e)
    return top, rows_sum(mass)


def lanes(pair, base=0):
    return slice(base + pair * LANES, base + (pair + 1) * LANES)


def score_head(level_ref, q_ref, k_ref, head):
    at = lanes(head // 2)
    queries = head_rows(q_ref[:, at].T, head % 2, LANES // 2)
    level_ref[...] = mm(k_ref[:, at], queries)


def near_kernel(me_ref, q_ref, kv_ref, ids_ref, ct_ref, st_ref, e_ref, bias_ref, level_ref):
    side = lax.rem(me_ref[0], 2)
    fill_bias(bias_ref, ids_ref, side, side)
    width = q_ref.shape[1]
    head_dim = LANES // 2
    unit = LOG2E / math.sqrt(head_dim)
    score_head(level_ref.at[0], q_ref, kv_ref, 0)
    for head in range(HEADS):
        if head + 1 < HEADS:
            score_head(level_ref.at[(head + 1) % 2], q_ref, kv_ref, head + 1)
        pair, which = head // 2, head % 2
        top, mass = softmax_head(level_ref.at[head % 2], bias_ref, unit, e_ref.at[head])
        values = kv_ref[:, lanes(pair, q_ref.shape[1])].T[which * head_dim : (which + 1) * head_dim]
        ct_ref[head * head_dim : (head + 1) * head_dim] = mm(values, e_ref[head])
        st_ref[pair, which : which + 1] = top
        st_ref[pair, 2 + which : 3 + which] = mass


def attend_near(me, q, kv, ids):
    rows, width = q.shape
    pairs = width // LANES
    return pl.pallas_call(
        near_kernel,
        in_specs=[SMEM] + [VMEM] * 3,
        out_specs=[VMEM] * 3,
        out_shape=[
            jax.ShapeDtypeStruct((width, rows), F32),
            jax.ShapeDtypeStruct((pairs, 8, rows), F32),
            jax.ShapeDtypeStruct((HEADS, rows, rows), BF16),
        ],
        scratch_shapes=[pltpu.VMEM((rows, rows), F32), pltpu.VMEM((2, rows, rows), F32)],
        compiler_params=params(6),
        cost_estimate=cost(8 * rows * rows * width, 3 * HEADS * rows * rows, HEADS * rows * rows),
        name="attend_near",
    )(me, q, kv, ids)


def far_kernel(
    me_ref,
    q_ref,
    came_hbm,
    ids_ref,
    cn_ref,
    sn_ref,
    kv_ref,
    c_ref,
    ct_ref,
    st_ref,
    e_ref,
    bias_ref,
    level_ref,
    sem,
):
    loads = []
    for i in range(2):
        span = pl.ds(i * q_ref.shape[1], q_ref.shape[1])
        loads.append(pltpu.make_async_copy(came_hbm.at[:, span], kv_ref.at[:, span], sem.at[i]))
        loads[i].start()
    side = lax.rem(me_ref[0], 2)
    fill_bias(bias_ref, ids_ref, 1 - side, side)
    head_dim = LANES // 2
    unit = LOG2E / math.sqrt(head_dim)
    loads[0].wait()
    score_head(level_ref.at[0], q_ref, kv_ref, 0)
    loads[1].wait()
    for head in range(HEADS):
        if head + 1 < HEADS:
            score_head(level_ref.at[(head + 1) % 2], q_ref, kv_ref, head + 1)
        pair, which = head // 2, head % 2
        near_top = sn_ref[pair, which : which + 1]
        near_mass = sn_ref[pair, 2 + which : 3 + which]
        top, mass = softmax_head(level_ref.at[head % 2], bias_ref, unit, e_ref.at[head], near_top)
        near_part = jnp.exp2(near_top - top)
        inverse = 1.0 / (mass + near_mass * near_part)
        values = kv_ref[:, lanes(pair, q_ref.shape[1])].T[which * head_dim : (which + 1) * head_dim]
        rows = slice(head * head_dim, (head + 1) * head_dim)
        ct_ref[rows] = (mm(values, e_ref[head]) + cn_ref[rows] * near_part) * inverse
        st_ref[pair, which : which + 1] = near_part * inverse
        st_ref[pair, 2 + which : 3 + which] = inverse
        if which:
            c_ref[:, lanes(pair)] = ct_ref[lanes(pair)].astype(BF16).T


def attend_far(me, q, came, ids, near_ct, near_st):
    rows, width = q.shape
    pairs = width // LANES
    return pl.pallas_call(
        far_kernel,
        in_specs=[SMEM, VMEM, HBM] + [VMEM] * 3,
        out_specs=[VMEM] * 5,
        out_shape=[
            jax.ShapeDtypeStruct((rows, 2 * width), BF16),
            jax.ShapeDtypeStruct((rows, width), BF16),
            jax.ShapeDtypeStruct((width, rows), F32),
            jax.ShapeDtypeStruct((pairs, 8, rows), F32),
            jax.ShapeDtypeStruct((HEADS, rows, rows), BF16),
        ],
        scratch_shapes=[
            pltpu.VMEM((rows, rows), F32),
            pltpu.VMEM((2, rows, rows), F32),
            pltpu.SemaphoreType.DMA((2,)),
        ],
        compiler_params=params(6),
        cost_estimate=cost(6 * rows * rows * width, 3 * HEADS * rows * rows, HEADS * rows * rows),
        name="attend_far",
    )(me, q, came, ids, near_ct, near_st)


def middle_kernel(
    me_ref,
    x_ref,
    og_ref,
    c_ref,
    wo_ref,
    fi_ref,
    fo_ref,
    d1_ref,
    bd1_ref,
    u1_ref,
    bu1_ref,
    d2_ref,
    bd2_ref,
    u2_ref,
    bu2_ref,
    g1_ref,
    b1_ref,
    g2_ref,
    b2_ref,
    out_hbm,
    df_ref,
    dc_ref,
    *rest,
):
    own_ref, other_ref, *scratch = rest
    (
        out_ref,
        sem,
        grad_ref,
        attn_ref,
        branch_ref,
        xhat_ref,
        rstd_ref,
        normed_ref,
        nb_ref,
        post_ref,
        pre_ref,
        act_ref,
        slope_ref,
    ) = scratch
    db_ref, acc_ref = nb_ref, branch_ref

    rows, width = x_ref.shape
    ff = fi_ref.shape[1]
    wide = pre_ref.shape[2]
    chunks = ff // wide
    none = jnp.zeros((8, width), F32)

    attn_ref[...] = mm(c_ref[...], wo_ref[...]).astype(BF16)
    hidden, slope_one = gelu_pair(mm(attn_ref[...], d1_ref[...], NT) + row(bd1_ref))
    hidden_one = hidden.astype(BF16)
    branch_ref[...] = mm(hidden_one, u1_ref[...])

    def first_norm(at, sums):
        x = x_ref[at].astype(F32)
        branch = branch_ref[at] + row(bu1_ref)
        xhat, rstd = norm_forward(x + attn_ref[at].astype(F32) + branch)
        normed = xhat * row(g1_ref) + row(b1_ref)
        xhat_ref[at] = xhat
        rstd_ref[at] = rstd
        normed_ref[at] = normed
        nb_ref[at] = normed.astype(BF16)
        terms = (branch * branch, x * x, normed * normed)
        return tuple(a + fold(b) for a, b in zip(sums, terms))

    branch_sq, input_sq, normed_sq = map(total, each_tile(rows, 32, first_norm, (none,) * 3))

    pre_ref[0] = mm(nb_ref[...], fi_ref[:, :wide])
    for j in range(chunks):
        if j + 1 < chunks:
            pre_ref[(j + 1) % 2] = mm(nb_ref[...], fi_ref[:, (j + 1) * wide : (j + 2) * wide])
        for r in range(0, rows, 16):
            act, slope = gelu_pair(pre_ref[j % 2, r : r + 16])
            act_ref[j % 2, r : r + 16] = act.astype(BF16)
            slope_ref[r : r + 16, j * wide : (j + 1) * wide] = slope.astype(BF16)
        part = mm(act_ref[j % 2], fo_ref[j * wide : (j + 1) * wide])
        if j == 0:
            acc_ref[...] = part
        else:
            acc_ref[...] += part

    post_ref[...] = acc_ref[...].astype(BF16)
    hidden, slope_two = gelu_pair(mm(post_ref[...], d2_ref[...], NT) + row(bd2_ref))
    hidden_two = hidden.astype(BF16)
    branch_ref[...] = mm(hidden_two, u2_ref[...])

    def second_norm(at, sums):
        branch = branch_ref[at] + row(bu2_ref)
        xhat, rstd = norm_forward(normed_ref[at] + post_ref[at].astype(F32) + branch)
        out_ref[at] = (xhat * row(g2_ref) + row(b2_ref)).astype(BF16)
        og = og_ref[at].astype(F32)
        d_second = norm_backward(xhat, rstd, og * row(g2_ref))
        d_branch = d_second.astype(BF16)
        normed_ref[at] = d_second
        db_ref[at] = d_branch
        terms = (branch * branch, og * xhat, og, d_branch.astype(F32))
        return tuple(a + fold(b) for a, b in zip(sums, terms))

    second_sq, gain2, bias2, up_bias2 = each_tile(rows, 32, second_norm, (none,) * 4)
    save = pltpu.make_async_copy(out_ref, out_hbm, sem)
    save.start()
    second_sq = total(second_sq)
    gain2, bias2, up_bias2 = map(rows_sum, (gain2, bias2, up_bias2))
    put_packed(grad_ref, 0, mm(hidden_two, db_ref[...], TN))
    d_pre = (mm(db_ref[...], u2_ref[...], NT) * slope_two).astype(BF16)
    put_packed(grad_ref, 1, mm(d_pre, post_ref[...], TN))
    down_bias2 = rows_sum(d_pre.astype(F32))
    post_ref[...] = (normed_ref[...] + mm(d_pre, d2_ref[...])).astype(BF16)

    pre_ref[0] = mm(post_ref[...], fo_ref[:wide], NT)
    for j in range(chunks):
        if j + 1 < chunks:
            pre_ref[(j + 1) % 2] = mm(post_ref[...], fo_ref[(j + 1) * wide : (j + 2) * wide], NT)
        for r in range(0, rows, 16):
            slope = slope_ref[r : r + 16, j * wide : (j + 1) * wide].astype(F32)
            act_ref[j % 2, r : r + 16] = (pre_ref[j % 2, r : r + 16] * slope).astype(BF16)
        part = mm(act_ref[j % 2], fi_ref[:, j * wide : (j + 1) * wide], NT)
        if j == 0:
            acc_ref[...] = part
        else:
            acc_ref[...] += part

    def first_back(at, sums):
        d_normed = normed_ref[at] + acc_ref[at]
        xhat = xhat_ref[at]
        d_first = norm_backward(xhat, rstd_ref[at], d_normed * row(g1_ref))
        d_branch = d_first.astype(BF16)
        df_ref[at] = d_first
        db_ref[at] = d_branch
        terms = (d_normed * xhat, d_normed, d_branch.astype(F32))
        return tuple(a + fold(b) for a, b in zip(sums, terms))

    gain1, bias1, up_bias1 = map(rows_sum, each_tile(rows, 32, first_back, (none,) * 3))
    put_packed(grad_ref, 2, mm(hidden_one, db_ref[...], TN))
    d_pre = (mm(db_ref[...], u1_ref[...], NT) * slope_one).astype(BF16)
    put_packed(grad_ref, 3, mm(d_pre, attn_ref[...], TN))
    down_bias1 = rows_sum(d_pre.astype(F32))
    d_attn = (df_ref[...] + mm(d_pre, d1_ref[...])).astype(BF16)
    dc_ref[...] = mm(d_attn, wo_ref[...], NT).astype(BF16)

    lane = lax.broadcasted_iota(jnp.int32, (1, LANES), 1)
    sums = jnp.where(lane == 0, branch_sq, 0.0)
    sums = jnp.where(lane == 1, input_sq, sums)
    sums = jnp.where(lane == 2, second_sq, sums)
    sums = jnp.where(lane == 3, normed_sq, sums)
    at = 4 * d1_ref.shape[0] * (width // LANES)
    grad_ref[at:] = jnp.zeros((grad_ref.shape[0] - at, LANES), F32)
    for vector in (up_bias1, up_bias2, gain1, bias1, gain2, bias2):
        for lo in range(0, width, LANES):
            grad_ref[at : at + 1] = vector[:, lo : lo + LANES]
            at += 1
    grad_ref[at : at + 1] = jnp.concatenate([down_bias1, down_bias2], axis=1)
    grad_ref[at + 1 : at + 2] = sums
    save.wait()
    half = grad_ref.shape[0] // 2
    side = lax.rem(me_ref[0], 2)
    own_ref[...] = grad_ref[pl.ds(pl.multiple_of(side * half, half), half), :]
    other_ref[...] = grad_ref[pl.ds(pl.multiple_of((1 - side) * half, half), half), :].astype(BF16)


def middle(x, og, ctx, out_weight, ffn_in, ffn_out, small, me, packed):
    rows, width = x.shape
    ff = ffn_in.shape[1]
    adapt = small[0].shape[0]
    vmem = pl.BlockSpec(memory_space=pltpu.VMEM)
    smem = pl.BlockSpec(memory_space=pltpu.SMEM)
    return pl.pallas_call(
        middle_kernel,
        in_specs=[smem] + [vmem] * (6 + len(small)),
        out_specs=[HBM] + [vmem] * 4,
        out_shape=[
            pltpu.HBM((rows, width), BF16),
            jax.ShapeDtypeStruct((rows, width), F32),
            jax.ShapeDtypeStruct((rows, width), BF16),
            jax.ShapeDtypeStruct((packed // 2, LANES), F32),
            jax.ShapeDtypeStruct((packed // 2, LANES), BF16),
        ],
        scratch_shapes=[
            pltpu.VMEM((rows, width), BF16),
            pltpu.SemaphoreType.DMA,
            pltpu.VMEM((packed, LANES), F32),
            pltpu.VMEM((rows, width), BF16),
            pltpu.VMEM((rows, width), F32),
            pltpu.VMEM((rows, width), F32),
            pltpu.VMEM((rows, 1), F32),
            pltpu.VMEM((rows, width), F32),
            pltpu.VMEM((rows, width), BF16),
            pltpu.VMEM((rows, width), BF16),
            pltpu.VMEM((2, rows, 512), F32),
            pltpu.VMEM((2, rows, 512), BF16),
            pltpu.VMEM((rows, ff), BF16),
        ],
        compiler_params=params(19),
        cost_estimate=cost(
            8 * rows * width * (ff + width), 4 * width * ff + 12 * rows * width, rows * ff
        ),
        name="middle",
    )(me, x, og, ctx, out_weight, ffn_in, ffn_out, *small)


def back_begin(n, pair, base, refs, dp_ref):
    dc_ref, ct_ref, st_ref, e_ref, kv_ref, q_ref = refs
    head_dim = LANES // 2
    at = lanes(pair)
    d_ctx = dc_ref[:, at].T.astype(F32)
    outs = []
    weighted = []
    for which in range(2):
        span = slice(which * head_dim, (which + 1) * head_dim)
        part = (d_ctx[span] * st_ref[pair, base + which : base + which + 1]).astype(BF16)
        weighted.append(part)
        outs.append(rows_sum(part.astype(F32) * ct_ref[at][span]))
    do_t = jnp.concatenate(weighted, axis=0)
    for which in range(2):
        values = kv_ref[:, lanes(pair, q_ref.shape[1])]
        dp_ref[n, which] = mm(values, head_rows(do_t, which, head_dim))
    return do_t.T, outs


def both_heads(left, right):
    half = LANES // 2
    return mm(
        jnp.concatenate(left, axis=1),
        jnp.concatenate([head_lanes(right, 0, half), head_lanes(right, 1, half)], axis=0),
    )


def back_scores(n, pair, outs, e_ref, dp_ref, ds_ref):
    rows = dp_ref.shape[2]
    for which in range(2):
        for r in range(0, rows, TILE):
            e = e_ref[2 * pair + which, r : r + TILE].astype(F32)
            d_scores = e * (dp_ref[n, which, r : r + TILE] - outs[which])
            ds_ref[n, which, r : r + TILE] = d_scores.astype(BF16)


def back_pairs(pairs, base, refs, dp_ref, ds_ref):
    e_ref, kv_ref, q_ref = refs[3:]
    head_dim = LANES // 2
    scale = 1.0 / math.sqrt(head_dim)
    begun = [back_begin(n, pair, base, refs, dp_ref) for n, pair in enumerate(pairs)]
    results = []
    for n, pair in enumerate(pairs):
        do, outs = begun[n]
        back_scores(n, pair, outs, e_ref, dp_ref, ds_ref)
        results.append(both_heads([e_ref[2 * pair], e_ref[2 * pair + 1]], do))
    for n, pair in enumerate(pairs):
        kt = kv_ref[:, lanes(pair)].T
        dq = [mm(kt[w * head_dim : (w + 1) * head_dim], ds_ref[n, w]) for w in range(2)]
        dk = both_heads([ds_ref[n, 0], ds_ref[n, 1]], q_ref[:, lanes(pair)])
        yield n, jnp.concatenate(dq, axis=0) * scale, dk * scale, results[n]


def back_far_kernel(pairs, *refs):
    ins, (dqt_ref, dkv_ref, dp_ref, ds_ref) = refs[:6], refs[6:]
    for n, dqt, dk, dv in back_pairs(pairs, 2, ins, dp_ref, ds_ref):
        dqt_ref[lanes(n)] = dqt
        dkv_ref[:, lanes(2 * n)] = dk.astype(BF16)
        dkv_ref[:, lanes(2 * n + 1)] = dv.astype(BF16)


def back_near_kernel(pairs, places, *refs):
    ins, (w_ref, begun_ref), refs = refs[:6], refs[6:8], refs[8:]
    shares, (out_ref, dp_ref, ds_ref, all_ref) = refs[:-4], refs[-4:]
    width = begun_ref.shape[1]
    count = len(pairs)
    for n, dqt, dk, dv in back_pairs(pairs, 0, ins, dp_ref, ds_ref):
        group, at = places[n]
        dqt_ref, came_ref = shares[2 * group : 2 * group + 2]
        all_ref[:, lanes(n)] = (dqt + dqt_ref[lanes(at)]).astype(BF16).T
        all_ref[:, lanes(count + n)] = (dk + came_ref[:, lanes(2 * at)].astype(F32)).astype(BF16)
        all_ref[:, lanes(2 * count + n)] = (
            dv + came_ref[:, lanes(2 * at + 1)].astype(F32)
        ).astype(BF16)
    columns = [lanes(pair, kind * width) for kind in range(3) for pair in pairs]
    weights = jnp.concatenate([w_ref[:, column] for column in columns], axis=1)
    out_ref[...] = (begun_ref[...] + mm(all_ref[...], weights, NT)).astype(out_ref.dtype)


def back_scratch(rows, count):
    return [
        pltpu.VMEM((count, 2, rows, rows), F32),
        pltpu.VMEM((count, 2, rows, rows), BF16),
    ]


def attend_back_far(pairs, d_ctx, ct, st, e, kv, q):
    rows, width = q.shape
    count = len(pairs)
    return pl.pallas_call(
        functools.partial(back_far_kernel, pairs),
        in_specs=[VMEM] * 6,
        out_specs=[VMEM] * 2,
        out_shape=[
            jax.ShapeDtypeStruct((count * LANES, rows), F32),
            jax.ShapeDtypeStruct((rows, 2 * count * LANES), BF16),
        ],
        scratch_shapes=back_scratch(rows, count),
        compiler_params=params(15),
        cost_estimate=cost(200 * rows * rows * LANES * count, 6 * rows * rows * count),
        name="back_far",
    )(d_ctx, ct, st, e, kv, q)


def attend_back_near(pairs, shares, dtype, d_ctx, ct, st, e, kv, q, weight, begun):
    rows, width = q.shape
    count = len(pairs)
    used = [group for group in shares if set(group) & set(pairs)]
    places = [
        next((i, group.index(pair)) for i, group in enumerate(used) if pair in group)
        for pair in pairs
    ]
    return pl.pallas_call(
        functools.partial(back_near_kernel, pairs, places),
        in_specs=[VMEM] * (8 + 2 * len(used)),
        out_specs=VMEM,
        out_shape=jax.ShapeDtypeStruct((rows, width), dtype),
        scratch_shapes=back_scratch(rows, count) + [pltpu.VMEM((rows, 3 * count * LANES), BF16)],
        compiler_params=params(16),
        cost_estimate=cost(300 * rows * rows * LANES * count, 6 * rows * rows * count),
        name="back_near",
    )(d_ctx, ct, st, e, kv, q, weight, begun, *(x for group in used for x in shares[group]))


def levels_of(devices):
    levels = []
    stride = 2
    while stride < devices:
        size = math.gcd(devices // stride, 4)
        levels.append((stride, size))
        stride *= size
    return levels


def trade(values, devices, level):
    stride, size = level
    came = []
    for s in range(1, size):
        moves = []
        for i in range(devices):
            pos = i // stride % size
            moves.append((i, i + ((pos + s) % size - pos) * stride))
        came.append(lax.ppermute(values[s - 1], ("dp", "seq"), moves))
    return came


def call_small(kernel, name, operands, shapes, scratch=()):
    specs = [VMEM if x.ndim > 1 else SMEM for x in operands]
    return pl.pallas_call(
        kernel,
        in_specs=specs,
        out_specs=[VMEM] * len(shapes),
        out_shape=shapes,
        scratch_shapes=list(scratch),
        compiler_params=params(6),
        cost_estimate=cost(operands[-1].size, 8 * operands[-1].size),
        name=name,
    )(*operands)


def place_of(me_ref, level):
    stride, size = level
    return lax.rem(lax.div(me_ref[0], stride), size)


def split_kernel(level, me_ref, own_ref, came_ref, *refs):
    outs, sum_ref = refs[:-1], refs[-1]
    sum_ref[...] = own_ref[...].astype(F32) + came_ref[...].astype(F32)
    rows = outs[0].shape[0]
    place = place_of(me_ref, level)
    for s, ref in enumerate(outs):
        at = lax.rem(place + s, level[1]) * rows
        ref[...] = sum_ref[pl.ds(pl.multiple_of(at, rows), rows), :].astype(BF16)


def add_split(me, own, came, level):
    rows, columns = own.shape
    return call_small(
        functools.partial(split_kernel, level),
        "add_split",
        (me, own, came),
        [jax.ShapeDtypeStruct((rows // level[1], columns), BF16)] * level[1],
        [pltpu.VMEM((rows, columns), F32)],
    )


def add_kernel(level, me_ref, *refs):
    ins, out_ref, all_ref = refs[:-2], refs[-2], refs[-1]
    place = place_of(me_ref, level)
    for s, ref in enumerate(ins):
        all_ref[lax.rem(place + level[1] - s, level[1])] = ref[...].astype(F32)
    value = all_ref[0]
    for s in range(1, len(ins)):
        value = value + all_ref[s]
    out_ref[...] = value.astype(BF16)


def add_group(me, values, level):
    shape = values[0].shape
    return call_small(
        functools.partial(add_kernel, level),
        "add_group",
        (me, *values),
        [jax.ShapeDtypeStruct(shape, BF16)],
        [pltpu.VMEM((level[1], *shape), F32)],
    )[0]


def join_kernel(level, me_ref, *refs):
    ins, out_ref, all_ref = refs[:-2], refs[-2], refs[-1]
    rows = ins[0].shape[0]
    place = place_of(me_ref, level)
    for s, ref in enumerate(ins):
        at = lax.rem(place + level[1] - s, level[1]) * rows
        all_ref[pl.ds(pl.multiple_of(at, rows), rows), :] = ref[...].astype(F32)
    out_ref[...] = all_ref[...].astype(BF16)


def join(me, values, level):
    rows, columns = values[0].shape
    rows = rows * level[1]
    return call_small(
        functools.partial(join_kernel, level),
        "join",
        (me, *values),
        [jax.ShapeDtypeStruct((rows, columns), BF16)],
        [pltpu.VMEM((rows, columns), F32)],
    )[0]


def unpack_kernel(me_ref, own_ref, came_ref, *refs):
    outs, all_ref = refs[:-1], refs[-1]
    half = own_ref.shape[0]
    side = lax.rem(me_ref[0], 2)
    for place, ref in ((side, own_ref), (1 - side, came_ref)):
        all_ref[pl.ds(pl.multiple_of(place * half, half), half), :] = ref[...].astype(F32)
    up2, down2, up1, down1, ub1, ub2, g1, b1, g2, b2, db1, db2, r1, r2 = outs
    adapt, width = up2.shape
    at = 0
    for ref in (up2, down2, up1, down1):
        for lo in range(0, width, LANES):
            ref[:, lo : lo + LANES] = all_ref[at : at + adapt]
            at += adapt
    for ref in (ub1, ub2, g1, b1, g2, b2):
        for lo in range(0, width, LANES):
            ref[lo : lo + LANES] = all_ref[at]
            at += 1
    biases = all_ref[at : at + 1]
    db1[...] = biases[:, :adapt]
    db2[...] = biases[:, adapt:]
    roots = jnp.sqrt(all_ref[at + 1 : at + 2])
    r1[...] = roots[:, 0:1] / roots[:, 1:2]
    r2[...] = roots[:, 2:3] / roots[:, 3:4]


def unpack(me, own, came, adapt, width):
    vmem = pl.BlockSpec(memory_space=pltpu.VMEM)
    shapes = [(adapt, width)] * 4 + [(width,)] * 6 + [(1, adapt)] * 2 + [(1, 1)] * 2
    return pl.pallas_call(
        unpack_kernel,
        in_specs=[pl.BlockSpec(memory_space=pltpu.SMEM), vmem, vmem],
        out_specs=[vmem] * len(shapes),
        out_shape=[jax.ShapeDtypeStruct(s, F32) for s in shapes],
        scratch_shapes=[pltpu.VMEM((2 * own.shape[0], LANES), F32)],
        compiler_params=params(6),
        cost_estimate=cost(4 * adapt * width, 24 * adapt * width),
        name="unpack",
    )(me, own, came)


def sum_stages(me, own, other, devices, adapt, width):
    cores = (1, 2)
    levels = levels_of(devices) or [(2, 1)]
    (came,) = trade([other], devices, cores)
    beside = yield
    parts = add_split(me, own, after(beside, came), levels[0])
    yield parts[0]
    came = trade(parts[1:], devices, levels[0])
    beside = yield
    own = add_group(me, [parts[0], *after(beside, came)], levels[0])
    yield own
    for level in levels[1:]:
        came = trade([own] * level[1], devices, level)
        beside = yield
        own = add_group(me, [own, *after(beside, came)], level)
        yield own
    came = trade([own] * levels[0][1], devices, levels[0])
    beside = yield
    own = join(me, [own, *after(beside, came)], levels[0])
    yield own
    (came,) = trade([own], devices, cores)
    beside = yield
    yield unpack(me, own, after(beside, came), adapt, width)
    while True:
        yield None


def beside(stages, kernel_result, operand, sums):
    done = stages.send(kernel_result)
    if done is None:
        return operand, sums
    operand = after(done, operand)
    next(stages)
    return operand, done


def after(done, value):
    return lax.optimization_barrier((value, done))[0]


def per_device(
    hidden_in,
    out_grad,
    segments,
    qkv_weight,
    out_weight,
    ffn_in,
    ffn_out,
    first_down,
    first_down_bias,
    first_up,
    first_up_bias,
    second_down,
    second_down_bias,
    second_up,
    second_up_bias,
    norm1_gain,
    norm1_bias,
    norm2_gain,
    norm2_bias,
):
    seqs, half, width = hidden_in.shape
    adapt = first_down.shape[1]
    assert seqs == 1
    x = hidden_in.reshape(half, width)
    og = out_grad.reshape(half, width)
    devices = lax.axis_size("dp") * 2
    me = (lax.axis_index("dp") * 2 + lax.axis_index("seq")).astype(jnp.int32).reshape(1)
    swap = [(0, 1), (1, 0)]

    kv, q = project(x, qkv_weight)
    kv_came = lax.ppermute(kv, "seq", swap)
    near_ct, near_st, near_e = attend_near(me, q, kv, segments)
    kv_far, ctx, ct, st, far_e = attend_far(me, q, kv_came, segments, near_ct, near_st)
    layer_out, d_first, d_ctx, own, other = middle(
        x,
        og,
        ctx,
        out_weight,
        ffn_in,
        ffn_out,
        (
            first_down.T,
            first_down_bias,
            first_up,
            first_up_bias,
            second_down.T,
            second_down_bias,
            second_up,
            second_up_bias,
            norm1_gain,
            norm1_bias,
            norm2_gain,
            norm2_bias,
        ),
        me,
        packed_rows(adapt, width),
    )
    stages = sum_stages(me, own, other, devices, adapt, width)
    next(stages)
    plan = (
        ((False, (0,)),),
        ((False, (1, 2, 3)),),
        ((False, (4, 5)), (True, (0, 1)),),
        ((True, (2, 3, 4)),),
        ((True, (5,)),),
    )
    sums = None
    shares = {}
    begun = d_first
    for line in plan:
        for near, pairs in line:
            if near:
                dtype = BF16 if line is plan[-1] else F32
                begun = attend_back_near(
                    pairs, shares, dtype, d_ctx, ct, st, near_e, kv, q, qkv_weight, begun
                )
                result = begun
            else:
                result, dkv = attend_back_far(pairs, d_ctx, ct, st, far_e, kv_far, q)
                shares[pairs] = (result, lax.ppermute(dkv, "seq", swap))
        st, sums = beside(stages, result, st, sums)
    input_grad = begun
    for unused in range(2 + devices.bit_length()):
        st, sums = beside(stages, begun, st, sums)
    up2, down2, up1, down1, ub1, ub2, g1, b1, g2, b2, db1, db2, r1, r2 = sums
    return (
        layer_out.reshape(1, half, width),
        input_grad.reshape(1, half, width),
        down1.T,
        db1.reshape(adapt),
        up1,
        ub1,
        down2.T,
        db2.reshape(adapt),
        up2,
        ub2,
        g1,
        b1,
        g2,
        b2,
        r1.reshape(()),
        r2.reshape(()),
    )


def solution(mesh):
    split = P("dp", "seq", None)
    return jax.shard_map(
        per_device,
        mesh=mesh,
        in_specs=(split, split, P("dp", None)) + (P(),) * 16,
        out_specs=(split, split) + (P(),) * 14,
        check_vma=False,
    )
```

```python
import functools
import math

import jax
import jax.numpy as jnp
from jax import lax
from jax.experimental import pallas as pl
from jax.experimental.pallas import tpu as pltpu
from jax.sharding import PartitionSpec as P

HEADS = 12
F32 = jnp.float32
BF16 = jnp.bfloat16
LOG2E = math.log2(math.e)
MASKED = -1.0e9
MIB = 1024 * 1024
LANES = 128
TILE = 32

NN = (((1,), (0,)), ((), ()))
NT = (((1,), (1,)), ((), ()))
TN = (((0,), (0,)), ((), ()))


def mm(left, right, dims=NN):
    return lax.dot_general(left, right, dims, preferred_element_type=F32)


def gelu_pair(v):
    cdf = 0.5 + 0.5 * lax.erf(v * math.sqrt(0.5))
    bell = jnp.exp2(v * v * (-0.5 * LOG2E))
    return v * cdf, cdf + v * bell * (1.0 / math.sqrt(2.0 * math.pi))


def row(ref):
    return ref[...].reshape(1, -1)


def rows_sum(value):
    return jnp.sum(value, axis=0, keepdims=True)


def lanes_mean(value):
    return jnp.mean(value, axis=-1, keepdims=True)


def fold(value):
    return jnp.sum(value.reshape(-1, 8, value.shape[-1]), axis=0)


def each_tile(rows, tile, body, sums):
    for at in range(rows.start, rows.stop, tile):
        sums = body(slice(at, at + tile), sums)
    return sums


def total(value):
    return jnp.sum(rows_sum(value), axis=1, keepdims=True)


def norm_forward(resid):
    center = resid - lanes_mean(resid)
    rstd = lax.rsqrt(lanes_mean(center * center) + 1e-12)
    return center * rstd, rstd


def packed_rows(adapt, width):
    rows = 4 * adapt * (width // LANES) + 6 * (width // LANES) + 2
    return -(-rows // 128) * 128


def put_packed(ref, number, value):
    rows, width = value.shape
    for i in range(width // LANES):
        at = (number * (width // LANES) + i) * rows
        ref[at : at + rows] = value[:, i * LANES : (i + 1) * LANES]


def norm_backward(xhat, rstd, dxhat):
    return rstd * (dxhat - lanes_mean(dxhat) - xhat * lanes_mean(dxhat * xhat))


def head_lanes(pair, which, head_dim):
    lane = lax.broadcasted_iota(jnp.int32, pair.shape, 1)
    keep = (lane < head_dim) if which == 0 else (lane >= head_dim)
    return jnp.where(keep, pair, jnp.zeros_like(pair))


def head_rows(pair, which, head_dim):
    part = pair[which * head_dim : (which + 1) * head_dim]
    blank = jnp.zeros_like(part)
    return jnp.concatenate([part, blank] if which == 0 else [blank, part], axis=0)


def params(vmem=20, **more):
    return pltpu.CompilerParams(vmem_limit_bytes=vmem * MIB, **more)


def cost(flops, moved, exps=0):
    return pl.CostEstimate(flops=int(flops), bytes_accessed=int(moved), transcendentals=int(exps))


def stay(*arrays):
    return [pltpu.with_memory_space_constraint(x, pltpu.HBM) for x in arrays]


def qkv_kernel(x_hbm, w_hbm, kv_ref, q_ref, x_ref, w_ref, sem):
    width = x_ref.shape[1]
    load_x = pltpu.make_async_copy(x_hbm, x_ref, sem.at[3])
    load_x.start()
    loads = []
    for i, part in enumerate((1, 2, 0)):
        span = pl.ds(part * width, width)
        loads.append(pltpu.make_async_copy(w_hbm.at[:, span], w_ref.at[i], sem.at[i]))
        loads[-1].start()
    load_x.wait()
    for i in range(2):
        loads[i].wait()
        kv_ref[:, i * width : (i + 1) * width] = mm(x_ref[...], w_ref[i]).astype(BF16)
    loads[2].wait()
    q_ref[...] = mm(x_ref[...], w_ref[2]).astype(BF16)


VMEM = pl.BlockSpec(memory_space=pltpu.VMEM)
SMEM = pl.BlockSpec(memory_space=pltpu.SMEM)
HBM = pl.BlockSpec(memory_space=pl.ANY)


def project(x, qkv_weight):
    rows, width = x.shape
    return pl.pallas_call(
        qkv_kernel,
        in_specs=[HBM, HBM],
        out_specs=[VMEM] * 2,
        out_shape=[
            jax.ShapeDtypeStruct((rows, 2 * width), BF16),
            jax.ShapeDtypeStruct((rows, width), BF16),
        ],
        scratch_shapes=[
            pltpu.VMEM((rows, width), BF16),
            pltpu.VMEM((3, width, width), BF16),
            pltpu.SemaphoreType.DMA((4,)),
        ],
        compiler_params=params(9),
        cost_estimate=cost(6 * rows * width * width, 6 * width * width),
        name="project",
    )(*stay(x, qkv_weight))


def fill_bias(bias_ref, ids_ref, key_side, query_side):
    half = bias_ref.shape[0]
    keys = ids_ref[:, pl.ds(pl.multiple_of(key_side * half, half), half)].astype(F32)
    queries = ids_ref[:, pl.ds(pl.multiple_of(query_side * half, half), half)].astype(F32)
    column = jnp.broadcast_to(keys, (LANES, half)).T
    for lo in range(0, half, LANES):
        bias_ref[:, lo : lo + LANES] = jnp.where(column == queries[:, lo : lo + LANES], 0.0, MASKED)


def softmax_head(level_ref, bias_ref, unit, e_ref, floor=None):
    rows, columns = level_ref.shape
    peak = None
    for r in range(0, rows, TILE):
        level = level_ref[r : r + TILE] * unit + bias_ref[r : r + TILE]
        level_ref[r : r + TILE] = level
        part = jnp.max(level.reshape(-1, 8, columns), axis=0)
        peak = part if peak is None else jnp.maximum(peak, part)
    top = jnp.max(peak, axis=0, keepdims=True)
    if floor is not None:
        top = jnp.maximum(top, floor)
    mass = None
    for r in range(0, rows, TILE):
        e = jnp.exp2(level_ref[r : r + TILE] - top)
        e_ref[r : r + TILE] = e.astype(BF16)
        mass = fold(e) if mass is None else mass + fold(e)
    return top, rows_sum(mass)


def lanes(pair, base=0):
    return slice(base + pair * LANES, base + (pair + 1) * LANES)


def score_head(level_ref, q_ref, k_ref, head):
    at = lanes(head // 2)
    queries = head_rows(q_ref[:, at].T, head % 2, LANES // 2)
    level_ref[...] = mm(k_ref[:, at], queries)


def near_kernel(me_ref, q_ref, kv_ref, ids_ref, ct_ref, st_ref, e_ref, bias_ref, level_ref):
    side = lax.rem(me_ref[0], 2)
    fill_bias(bias_ref, ids_ref, side, side)
    width = q_ref.shape[1]
    head_dim = LANES // 2
    unit = LOG2E / math.sqrt(head_dim)
    score_head(level_ref.at[0], q_ref, kv_ref, 0)
    for head in range(HEADS):
        if head + 1 < HEADS:
            score_head(level_ref.at[(head + 1) % 2], q_ref, kv_ref, head + 1)
        pair, which = head // 2, head % 2
        top, mass = softmax_head(level_ref.at[head % 2], bias_ref, unit, e_ref.at[head])
        values = kv_ref[:, lanes(pair, q_ref.shape[1])].T[which * head_dim : (which + 1) * head_dim]
        ct_ref[head * head_dim : (head + 1) * head_dim] = mm(values, e_ref[head])
        st_ref[pair, which : which + 1] = top
        st_ref[pair, 2 + which : 3 + which] = mass


def attend_near(me, q, kv, ids):
    rows, width = q.shape
    pairs = width // LANES
    return pl.pallas_call(
        near_kernel,
        in_specs=[SMEM] + [VMEM] * 3,
        out_specs=[VMEM] * 3,
        out_shape=[
            jax.ShapeDtypeStruct((width, rows), F32),
            jax.ShapeDtypeStruct((pairs, 8, rows), F32),
            jax.ShapeDtypeStruct((HEADS, rows, rows), BF16),
        ],
        scratch_shapes=[pltpu.VMEM((rows, rows), F32), pltpu.VMEM((2, rows, rows), F32)],
        compiler_params=params(6),
        cost_estimate=cost(8 * rows * rows * width, 3 * HEADS * rows * rows, HEADS * rows * rows),
        name="attend_near",
    )(me, q, kv, ids)


def far_kernel(
    me_ref,
    q_ref,
    came_hbm,
    ids_ref,
    cn_ref,
    sn_ref,
    kv_ref,
    c_ref,
    ct_ref,
    st_ref,
    e_ref,
    bias_ref,
    level_ref,
    sem,
):
    loads = []
    for i in range(2):
        span = pl.ds(i * q_ref.shape[1], q_ref.shape[1])
        loads.append(pltpu.make_async_copy(came_hbm.at[:, span], kv_ref.at[:, span], sem.at[i]))
        loads[i].start()
    side = lax.rem(me_ref[0], 2)
    fill_bias(bias_ref, ids_ref, 1 - side, side)
    head_dim = LANES // 2
    unit = LOG2E / math.sqrt(head_dim)
    loads[0].wait()
    score_head(level_ref.at[0], q_ref, kv_ref, 0)
    loads[1].wait()
    for head in range(HEADS):
        if head + 1 < HEADS:
            score_head(level_ref.at[(head + 1) % 2], q_ref, kv_ref, head + 1)
        pair, which = head // 2, head % 2
        near_top = sn_ref[pair, which : which + 1]
        near_mass = sn_ref[pair, 2 + which : 3 + which]
        top, mass = softmax_head(level_ref.at[head % 2], bias_ref, unit, e_ref.at[head], near_top)
        near_part = jnp.exp2(near_top - top)
        inverse = 1.0 / (mass + near_mass * near_part)
        values = kv_ref[:, lanes(pair, q_ref.shape[1])].T[which * head_dim : (which + 1) * head_dim]
        rows = slice(head * head_dim, (head + 1) * head_dim)
        ct_ref[rows] = (mm(values, e_ref[head]) + cn_ref[rows] * near_part) * inverse
        st_ref[pair, which : which + 1] = near_part * inverse
        st_ref[pair, 2 + which : 3 + which] = inverse
        if which:
            c_ref[:, lanes(pair)] = ct_ref[lanes(pair)].astype(BF16).T


def attend_far(me, q, came, ids, near_ct, near_st):
    rows, width = q.shape
    pairs = width // LANES
    return pl.pallas_call(
        far_kernel,
        in_specs=[SMEM, VMEM, HBM] + [VMEM] * 3,
        out_specs=[VMEM] * 5,
        out_shape=[
            jax.ShapeDtypeStruct((rows, 2 * width), BF16),
            jax.ShapeDtypeStruct((rows, width), BF16),
            jax.ShapeDtypeStruct((width, rows), F32),
            jax.ShapeDtypeStruct((pairs, 8, rows), F32),
            jax.ShapeDtypeStruct((HEADS, rows, rows), BF16),
        ],
        scratch_shapes=[
            pltpu.VMEM((rows, rows), F32),
            pltpu.VMEM((2, rows, rows), F32),
            pltpu.SemaphoreType.DMA((2,)),
        ],
        compiler_params=params(6),
        cost_estimate=cost(6 * rows * rows * width, 3 * HEADS * rows * rows, HEADS * rows * rows),
        name="attend_far",
    )(me, q, came, ids, near_ct, near_st)


def middle_kernel(
    me_ref,
    x_ref,
    og_ref,
    c_ref,
    wo_ref,
    fi_ref,
    fo_ref,
    d1_ref,
    bd1_ref,
    u1_ref,
    bu1_ref,
    d2_ref,
    bd2_ref,
    u2_ref,
    bu2_ref,
    g1_ref,
    b1_ref,
    g2_ref,
    b2_ref,
    out_hbm,
    df_ref,
    dc_ref,
    *rest,
):
    own_ref, other_ref, *scratch = rest
    (
        out_ref,
        sem,
        grad_ref,
        attn_ref,
        branch_ref,
        xhat_ref,
        rstd_ref,
        normed_ref,
        nb_ref,
        post_ref,
        pre_ref,
        act_ref,
        slope_ref,
    ) = scratch
    db_ref, acc_ref = nb_ref, branch_ref

    rows, width = x_ref.shape
    ff = fi_ref.shape[1]
    wide = pre_ref.shape[2]
    chunks = ff // wide
    none = jnp.zeros((8, width), F32)
    halves = (slice(0, rows // 2), slice(rows // 2, rows))

    ones = []
    for half in halves:
        attn_ref[half] = mm(c_ref[half], wo_ref[...]).astype(BF16)
        hidden, slope = gelu_pair(mm(attn_ref[half], d1_ref[...], NT) + row(bd1_ref))
        ones.append((hidden.astype(BF16), slope))
        branch_ref[half] = mm(ones[-1][0], u1_ref[...])
    hidden_one, slope_one = (jnp.concatenate(x, axis=0) for x in zip(*ones))

    def first_norm(at, sums):
        x = x_ref[at].astype(F32)
        branch = branch_ref[at] + row(bu1_ref)
        xhat, rstd = norm_forward(x + attn_ref[at].astype(F32) + branch)
        normed = xhat * row(g1_ref) + row(b1_ref)
        xhat_ref[at] = xhat
        rstd_ref[at] = rstd
        normed_ref[at] = normed
        nb_ref[at] = normed.astype(BF16)
        terms = (branch * branch, x * x, normed * normed)
        return tuple(a + fold(b) for a, b in zip(sums, terms))

    sums = (none,) * 3
    for half in halves:
        sums = each_tile(half, 32, first_norm, sums)
        pre_ref[0, half] = mm(nb_ref[half], fi_ref[:, :wide])
    branch_sq, input_sq, normed_sq = map(total, sums)

    for j in range(chunks):
        if j + 1 < chunks:
            pre_ref[(j + 1) % 2] = mm(nb_ref[...], fi_ref[:, (j + 1) * wide : (j + 2) * wide])
        for r in range(0, rows, 16):
            act, slope = gelu_pair(pre_ref[j % 2, r : r + 16])
            act_ref[j % 2, r : r + 16] = act.astype(BF16)
            slope_ref[r : r + 16, j * wide : (j + 1) * wide] = slope.astype(BF16)
        if j + 1 < chunks:
            part = mm(act_ref[j % 2], fo_ref[j * wide : (j + 1) * wide])
            if j == 0:
                acc_ref[...] = part
            else:
                acc_ref[...] += part

    twos = []
    for half in halves:
        last = mm(act_ref[(chunks - 1) % 2, half], fo_ref[ff - wide :])
        post_ref[half] = (acc_ref[half] + last).astype(BF16)
        hidden, slope = gelu_pair(mm(post_ref[half], d2_ref[...], NT) + row(bd2_ref))
        twos.append((hidden.astype(BF16), slope))
        branch_ref[half] = mm(twos[-1][0], u2_ref[...])
    hidden_two, slope_two = (jnp.concatenate(x, axis=0) for x in zip(*twos))

    def second_norm(at, sums):
        branch = branch_ref[at] + row(bu2_ref)
        xhat, rstd = norm_forward(normed_ref[at] + post_ref[at].astype(F32) + branch)
        out_ref[at] = (xhat * row(g2_ref) + row(b2_ref)).astype(BF16)
        og = og_ref[at].astype(F32)
        d_second = norm_backward(xhat, rstd, og * row(g2_ref))
        d_branch = d_second.astype(BF16)
        normed_ref[at] = d_second
        db_ref[at] = d_branch
        terms = (branch * branch, og * xhat, og, d_branch.astype(F32))
        return tuple(a + fold(b) for a, b in zip(sums, terms))

    sums = (none,) * 4
    d_pres = []
    for half, (unused, slope) in zip(halves, twos):
        sums = each_tile(half, 32, second_norm, sums)
        d_pres.append((mm(db_ref[half], u2_ref[...], NT) * slope).astype(BF16))
    second_sq, gain2, bias2, up_bias2 = sums
    save = pltpu.make_async_copy(out_ref, out_hbm, sem)
    save.start()
    second_sq = total(second_sq)
    gain2, bias2, up_bias2 = map(rows_sum, (gain2, bias2, up_bias2))
    put_packed(grad_ref, 0, mm(hidden_two, db_ref[...], TN))
    d_pre = jnp.concatenate(d_pres, axis=0)
    put_packed(grad_ref, 1, mm(d_pre, post_ref[...], TN))
    down_bias2 = rows_sum(d_pre.astype(F32))
    post_ref[...] = (normed_ref[...] + mm(d_pre, d2_ref[...])).astype(BF16)

    pre_ref[0] = mm(post_ref[...], fo_ref[:wide], NT)
    for j in range(chunks):
        if j + 1 < chunks:
            pre_ref[(j + 1) % 2] = mm(post_ref[...], fo_ref[(j + 1) * wide : (j + 2) * wide], NT)
        for r in range(0, rows, 16):
            slope = slope_ref[r : r + 16, j * wide : (j + 1) * wide].astype(F32)
            act_ref[j % 2, r : r + 16] = (pre_ref[j % 2, r : r + 16] * slope).astype(BF16)
        if j + 1 < chunks:
            part = mm(act_ref[j % 2], fi_ref[:, j * wide : (j + 1) * wide], NT)
            if j == 0:
                acc_ref[...] = part
            else:
                acc_ref[...] += part

    def first_back(at, sums):
        d_normed = normed_ref[at] + acc_ref[at]
        xhat = xhat_ref[at]
        d_first = norm_backward(xhat, rstd_ref[at], d_normed * row(g1_ref))
        d_branch = d_first.astype(BF16)
        df_ref[at] = d_first
        db_ref[at] = d_branch
        terms = (d_normed * xhat, d_normed, d_branch.astype(F32))
        return tuple(a + fold(b) for a, b in zip(sums, terms))

    sums = (none,) * 3
    d_pres = []
    for half, (unused, slope) in zip(halves, ones):
        acc_ref[half] += mm(act_ref[(chunks - 1) % 2, half], fi_ref[:, ff - wide :], NT)
        sums = each_tile(half, 32, first_back, sums)
        d_pre = (mm(db_ref[half], u1_ref[...], NT) * slope).astype(BF16)
        d_pres.append(d_pre)
        d_attn = (df_ref[half] + mm(d_pre, d1_ref[...])).astype(BF16)
        dc_ref[half] = mm(d_attn, wo_ref[...], NT).astype(BF16)
    gain1, bias1, up_bias1 = map(rows_sum, sums)
    put_packed(grad_ref, 2, mm(hidden_one, db_ref[...], TN))
    d_pre = jnp.concatenate(d_pres, axis=0)
    put_packed(grad_ref, 3, mm(d_pre, attn_ref[...], TN))
    down_bias1 = rows_sum(d_pre.astype(F32))

    lane = lax.broadcasted_iota(jnp.int32, (1, LANES), 1)
    sums = jnp.where(lane == 0, branch_sq, 0.0)
    sums = jnp.where(lane == 1, input_sq, sums)
    sums = jnp.where(lane == 2, second_sq, sums)
    sums = jnp.where(lane == 3, normed_sq, sums)
    at = 4 * d1_ref.shape[0] * (width // LANES)
    grad_ref[at:] = jnp.zeros((grad_ref.shape[0] - at, LANES), F32)
    for vector in (up_bias1, up_bias2, gain1, bias1, gain2, bias2):
        for lo in range(0, width, LANES):
            grad_ref[at : at + 1] = vector[:, lo : lo + LANES]
            at += 1
    grad_ref[at : at + 1] = jnp.concatenate([down_bias1, down_bias2], axis=1)
    grad_ref[at + 1 : at + 2] = sums
    save.wait()
    half = grad_ref.shape[0] // 2
    side = lax.rem(me_ref[0], 2)
    own_ref[...] = grad_ref[pl.ds(pl.multiple_of(side * half, half), half), :]
    other_ref[...] = grad_ref[pl.ds(pl.multiple_of((1 - side) * half, half), half), :].astype(BF16)


def middle(x, og, ctx, out_weight, ffn_in, ffn_out, small, me, packed):
    rows, width = x.shape
    ff = ffn_in.shape[1]
    adapt = small[0].shape[0]
    vmem = pl.BlockSpec(memory_space=pltpu.VMEM)
    smem = pl.BlockSpec(memory_space=pltpu.SMEM)
    return pl.pallas_call(
        middle_kernel,
        in_specs=[smem] + [vmem] * (6 + len(small)),
        out_specs=[HBM] + [vmem] * 4,
        out_shape=[
            pltpu.HBM((rows, width), BF16),
            jax.ShapeDtypeStruct((rows, width), F32),
            jax.ShapeDtypeStruct((rows, width), BF16),
            jax.ShapeDtypeStruct((packed // 2, LANES), F32),
            jax.ShapeDtypeStruct((packed // 2, LANES), BF16),
        ],
        scratch_shapes=[
            pltpu.VMEM((rows, width), BF16),
            pltpu.SemaphoreType.DMA,
            pltpu.VMEM((packed, LANES), F32),
            pltpu.VMEM((rows, width), BF16),
            pltpu.VMEM((rows, width), F32),
            pltpu.VMEM((rows, width), F32),
            pltpu.VMEM((rows, 1), F32),
            pltpu.VMEM((rows, width), F32),
            pltpu.VMEM((rows, width), BF16),
            pltpu.VMEM((rows, width), BF16),
            pltpu.VMEM((2, rows, 512), F32),
            pltpu.VMEM((2, rows, 512), BF16),
            pltpu.VMEM((rows, ff), BF16),
        ],
        compiler_params=params(19),
        cost_estimate=cost(
            8 * rows * width * (ff + width), 4 * width * ff + 12 * rows * width, rows * ff
        ),
        name="middle",
    )(me, x, og, ctx, out_weight, ffn_in, ffn_out, *small)


def back_begin(n, pair, base, refs, dp_ref):
    dc_ref, ct_ref, st_ref, e_ref, kv_ref, q_ref = refs
    head_dim = LANES // 2
    at = lanes(pair)
    d_ctx = dc_ref[:, at].T.astype(F32)
    outs = []
    weighted = []
    for which in range(2):
        span = slice(which * head_dim, (which + 1) * head_dim)
        part = (d_ctx[span] * st_ref[pair, base + which : base + which + 1]).astype(BF16)
        weighted.append(part)
        outs.append(rows_sum(part.astype(F32) * ct_ref[at][span]))
    do_t = jnp.concatenate(weighted, axis=0)
    for which in range(2):
        values = kv_ref[:, lanes(pair, q_ref.shape[1])]
        dp_ref[n, which] = mm(values, head_rows(do_t, which, head_dim))
    return do_t.T, outs


def both_heads(left, right):
    half = LANES // 2
    return mm(
        jnp.concatenate(left, axis=1),
        jnp.concatenate([head_lanes(right, 0, half), head_lanes(right, 1, half)], axis=0),
    )


def back_scores(n, pair, outs, e_ref, dp_ref, ds_ref):
    rows = dp_ref.shape[2]
    for which in range(2):
        for r in range(0, rows, TILE):
            e = e_ref[2 * pair + which, r : r + TILE].astype(F32)
            d_scores = e * (dp_ref[n, which, r : r + TILE] - outs[which])
            ds_ref[n, which, r : r + TILE] = d_scores.astype(BF16)


def back_pairs(pairs, base, refs, dp_ref, ds_ref):
    e_ref, kv_ref, q_ref = refs[3:]
    head_dim = LANES // 2
    scale = 1.0 / math.sqrt(head_dim)
    begun = [back_begin(n, pair, base, refs, dp_ref) for n, pair in enumerate(pairs)]
    results = []
    for n, pair in enumerate(pairs):
        do, outs = begun[n]
        back_scores(n, pair, outs, e_ref, dp_ref, ds_ref)
        results.append(both_heads([e_ref[2 * pair], e_ref[2 * pair + 1]], do))
    for n, pair in enumerate(pairs):
        kt = kv_ref[:, lanes(pair)].T
        dq = [mm(kt[w * head_dim : (w + 1) * head_dim], ds_ref[n, w]) for w in range(2)]
        dk = both_heads([ds_ref[n, 0], ds_ref[n, 1]], q_ref[:, lanes(pair)])
        yield n, jnp.concatenate(dq, axis=0) * scale, dk * scale, results[n]


def back_far_kernel(pairs, *refs):
    ins, (dqt_ref, dkv_ref, dp_ref, ds_ref) = refs[:6], refs[6:]
    for n, dqt, dk, dv in back_pairs(pairs, 2, ins, dp_ref, ds_ref):
        dqt_ref[lanes(n)] = dqt
        dkv_ref[:, lanes(2 * n)] = dk.astype(BF16)
        dkv_ref[:, lanes(2 * n + 1)] = dv.astype(BF16)


def back_near_kernel(pairs, places, *refs):
    ins, (w_ref, begun_ref), refs = refs[:6], refs[6:8], refs[8:]
    shares, (out_ref, dp_ref, ds_ref, all_ref) = refs[:-4], refs[-4:]
    width = begun_ref.shape[1]
    count = len(pairs)
    for n, dqt, dk, dv in back_pairs(pairs, 0, ins, dp_ref, ds_ref):
        group, at = places[n]
        dqt_ref, came_ref = shares[2 * group : 2 * group + 2]
        all_ref[:, lanes(n)] = (dqt + dqt_ref[lanes(at)]).astype(BF16).T
        all_ref[:, lanes(count + n)] = (dk + came_ref[:, lanes(2 * at)].astype(F32)).astype(BF16)
        all_ref[:, lanes(2 * count + n)] = (
            dv + came_ref[:, lanes(2 * at + 1)].astype(F32)
        ).astype(BF16)
    columns = [lanes(pair, kind * width) for kind in range(3) for pair in pairs]
    weights = jnp.concatenate([w_ref[:, column] for column in columns], axis=1)
    out_ref[...] = (begun_ref[...] + mm(all_ref[...], weights, NT)).astype(out_ref.dtype)


def back_scratch(rows, count):
    return [
        pltpu.VMEM((count, 2, rows, rows), F32),
        pltpu.VMEM((count, 2, rows, rows), BF16),
    ]


def attend_back_far(pairs, d_ctx, ct, st, e, kv, q):
    rows, width = q.shape
    count = len(pairs)
    return pl.pallas_call(
        functools.partial(back_far_kernel, pairs),
        in_specs=[VMEM] * 6,
        out_specs=[VMEM] * 2,
        out_shape=[
            jax.ShapeDtypeStruct((count * LANES, rows), F32),
            jax.ShapeDtypeStruct((rows, 2 * count * LANES), BF16),
        ],
        scratch_shapes=back_scratch(rows, count),
        compiler_params=params(15),
        cost_estimate=cost(200 * rows * rows * LANES * count, 6 * rows * rows * count),
        name="back_far",
    )(d_ctx, ct, st, e, kv, q)


def attend_back_near(pairs, shares, dtype, d_ctx, ct, st, e, kv, q, weight, begun):
    rows, width = q.shape
    count = len(pairs)
    used = [group for group in shares if set(group) & set(pairs)]
    places = [
        next((i, group.index(pair)) for i, group in enumerate(used) if pair in group)
        for pair in pairs
    ]
    return pl.pallas_call(
        functools.partial(back_near_kernel, pairs, places),
        in_specs=[VMEM] * (8 + 2 * len(used)),
        out_specs=VMEM,
        out_shape=jax.ShapeDtypeStruct((rows, width), dtype),
        scratch_shapes=back_scratch(rows, count) + [pltpu.VMEM((rows, 3 * count * LANES), BF16)],
        compiler_params=params(16),
        cost_estimate=cost(300 * rows * rows * LANES * count, 6 * rows * rows * count),
        name="back_near",
    )(d_ctx, ct, st, e, kv, q, weight, begun, *(x for group in used for x in shares[group]))


def levels_of(devices):
    levels = []
    stride = 2
    while stride < devices:
        size = math.gcd(devices // stride, 4)
        levels.append((stride, size))
        stride *= size
    return levels


def trade(values, devices, level):
    stride, size = level
    came = []
    for s in range(1, size):
        moves = []
        for i in range(devices):
            pos = i // stride % size
            moves.append((i, i + ((pos + s) % size - pos) * stride))
        came.append(lax.ppermute(values[s - 1], ("dp", "seq"), moves))
    return came


def call_small(kernel, name, operands, shapes, scratch=()):
    specs = [VMEM if x.ndim > 1 else SMEM for x in operands]
    return pl.pallas_call(
        kernel,
        in_specs=specs,
        out_specs=[VMEM] * len(shapes),
        out_shape=shapes,
        scratch_shapes=list(scratch),
        compiler_params=params(6),
        cost_estimate=cost(operands[-1].size, 8 * operands[-1].size),
        name=name,
    )(*operands)


def place_of(me_ref, level):
    stride, size = level
    return lax.rem(lax.div(me_ref[0], stride), size)


def split_kernel(level, me_ref, own_ref, came_ref, *refs):
    outs, sum_ref = refs[:-1], refs[-1]
    sum_ref[...] = own_ref[...].astype(F32) + came_ref[...].astype(F32)
    rows = outs[0].shape[0]
    place = place_of(me_ref, level)
    for s, ref in enumerate(outs):
        at = lax.rem(place + s, level[1]) * rows
        ref[...] = sum_ref[pl.ds(pl.multiple_of(at, rows), rows), :].astype(BF16)


def add_split(me, own, came, level):
    rows, columns = own.shape
    return call_small(
        functools.partial(split_kernel, level),
        "add_split",
        (me, own, came),
        [jax.ShapeDtypeStruct((rows // level[1], columns), BF16)] * level[1],
        [pltpu.VMEM((rows, columns), F32)],
    )


def add_kernel(level, me_ref, *refs):
    ins, out_ref, all_ref = refs[:-2], refs[-2], refs[-1]
    place = place_of(me_ref, level)
    for s, ref in enumerate(ins):
        all_ref[lax.rem(place + level[1] - s, level[1])] = ref[...].astype(F32)
    value = all_ref[0]
    for s in range(1, len(ins)):
        value = value + all_ref[s]
    out_ref[...] = value.astype(BF16)


def add_group(me, values, level):
    shape = values[0].shape
    return call_small(
        functools.partial(add_kernel, level),
        "add_group",
        (me, *values),
        [jax.ShapeDtypeStruct(shape, BF16)],
        [pltpu.VMEM((level[1], *shape), F32)],
    )[0]


def join_kernel(level, me_ref, *refs):
    ins, out_ref, all_ref = refs[:-2], refs[-2], refs[-1]
    rows = ins[0].shape[0]
    place = place_of(me_ref, level)
    for s, ref in enumerate(ins):
        at = lax.rem(place + level[1] - s, level[1]) * rows
        all_ref[pl.ds(pl.multiple_of(at, rows), rows), :] = ref[...].astype(F32)
    out_ref[...] = all_ref[...].astype(BF16)


def join(me, values, level):
    rows, columns = values[0].shape
    rows = rows * level[1]
    return call_small(
        functools.partial(join_kernel, level),
        "join",
        (me, *values),
        [jax.ShapeDtypeStruct((rows, columns), BF16)],
        [pltpu.VMEM((rows, columns), F32)],
    )[0]


def unpack_kernel(me_ref, own_ref, came_ref, *refs):
    outs, all_ref = refs[:-1], refs[-1]
    half = own_ref.shape[0]
    side = lax.rem(me_ref[0], 2)
    for place, ref in ((side, own_ref), (1 - side, came_ref)):
        all_ref[pl.ds(pl.multiple_of(place * half, half), half), :] = ref[...].astype(F32)
    up2, down2, up1, down1, ub1, ub2, g1, b1, g2, b2, db1, db2, r1, r2 = outs
    adapt, width = up2.shape
    at = 0
    for ref in (up2, down2, up1, down1):
        for lo in range(0, width, LANES):
            ref[:, lo : lo + LANES] = all_ref[at : at + adapt]
            at += adapt
    for ref in (ub1, ub2, g1, b1, g2, b2):
        for lo in range(0, width, LANES):
            ref[lo : lo + LANES] = all_ref[at]
            at += 1
    biases = all_ref[at : at + 1]
    db1[...] = biases[:, :adapt]
    db2[...] = biases[:, adapt:]
    roots = jnp.sqrt(all_ref[at + 1 : at + 2])
    r1[...] = roots[:, 0:1] / roots[:, 1:2]
    r2[...] = roots[:, 2:3] / roots[:, 3:4]


def unpack(me, own, came, adapt, width):
    vmem = pl.BlockSpec(memory_space=pltpu.VMEM)
    shapes = [(adapt, width)] * 4 + [(width,)] * 6 + [(1, adapt)] * 2 + [(1, 1)] * 2
    return pl.pallas_call(
        unpack_kernel,
        in_specs=[pl.BlockSpec(memory_space=pltpu.SMEM), vmem, vmem],
        out_specs=[vmem] * len(shapes),
        out_shape=[jax.ShapeDtypeStruct(s, F32) for s in shapes],
        scratch_shapes=[pltpu.VMEM((2 * own.shape[0], LANES), F32)],
        compiler_params=params(6),
        cost_estimate=cost(4 * adapt * width, 24 * adapt * width),
        name="unpack",
    )(me, own, came)


def sum_stages(me, own, other, devices, adapt, width):
    cores = (1, 2)
    levels = levels_of(devices) or [(2, 1)]
    (came,) = trade([other], devices, cores)
    beside = yield
    parts = add_split(me, own, after(beside, came), levels[0])
    yield parts[0]
    came = trade(parts[1:], devices, levels[0])
    beside = yield
    own = add_group(me, [parts[0], *after(beside, came)], levels[0])
    yield own
    for level in levels[1:]:
        came = trade([own] * level[1], devices, level)
        beside = yield
        own = add_group(me, [own, *after(beside, came)], level)
        yield own
    came = trade([own] * levels[0][1], devices, levels[0])
    beside = yield
    own = join(me, [own, *after(beside, came)], levels[0])
    yield own
    (came,) = trade([own], devices, cores)
    beside = yield
    yield unpack(me, own, after(beside, came), adapt, width)
    while True:
        yield None


def beside(stages, kernel_result, operand, sums):
    done = stages.send(kernel_result)
    if done is None:
        return operand, sums
    operand = after(done, operand)
    next(stages)
    return operand, done


def after(done, value):
    return lax.optimization_barrier((value, done))[0]


def per_device(
    hidden_in,
    out_grad,
    segments,
    qkv_weight,
    out_weight,
    ffn_in,
    ffn_out,
    first_down,
    first_down_bias,
    first_up,
    first_up_bias,
    second_down,
    second_down_bias,
    second_up,
    second_up_bias,
    norm1_gain,
    norm1_bias,
    norm2_gain,
    norm2_bias,
):
    seqs, half, width = hidden_in.shape
    adapt = first_down.shape[1]
    assert seqs == 1
    x = hidden_in.reshape(half, width)
    og = out_grad.reshape(half, width)
    devices = lax.axis_size("dp") * 2
    me = (lax.axis_index("dp") * 2 + lax.axis_index("seq")).astype(jnp.int32).reshape(1)
    swap = [(0, 1), (1, 0)]

    kv, q = project(x, qkv_weight)
    kv_came = lax.ppermute(kv, "seq", swap)
    near_ct, near_st, near_e = attend_near(me, q, kv, segments)
    kv_far, ctx, ct, st, far_e = attend_far(me, q, kv_came, segments, near_ct, near_st)
    layer_out, d_first, d_ctx, own, other = middle(
        x,
        og,
        ctx,
        out_weight,
        ffn_in,
        ffn_out,
        (
            first_down.T,
            first_down_bias,
            first_up,
            first_up_bias,
            second_down.T,
            second_down_bias,
            second_up,
            second_up_bias,
            norm1_gain,
            norm1_bias,
            norm2_gain,
            norm2_bias,
        ),
        me,
        packed_rows(adapt, width),
    )
    stages = sum_stages(me, own, other, devices, adapt, width)
    next(stages)
    plan = (
        ((False, (0,)),),
        ((False, (1, 2, 3)),),
        ((False, (4, 5)), (True, (0, 1)),),
        ((True, (2, 3, 4)),),
        ((True, (5,)),),
    )
    sums = None
    shares = {}
    begun = d_first
    for line in plan:
        for near, pairs in line:
            if near:
                dtype = BF16 if line is plan[-1] else F32
                begun = attend_back_near(
                    pairs, shares, dtype, d_ctx, ct, st, near_e, kv, q, qkv_weight, begun
                )
                result = begun
            else:
                result, dkv = attend_back_far(pairs, d_ctx, ct, st, far_e, kv_far, q)
                shares[pairs] = (result, lax.ppermute(dkv, "seq", swap))
        st, sums = beside(stages, result, st, sums)
    input_grad = begun
    for unused in range(2 + devices.bit_length()):
        st, sums = beside(stages, begun, st, sums)
    up2, down2, up1, down1, ub1, ub2, g1, b1, g2, b2, db1, db2, r1, r2 = sums
    return (
        layer_out.reshape(1, half, width),
        input_grad.reshape(1, half, width),
        down1.T,
        db1.reshape(adapt),
        up1,
        ub1,
        down2.T,
        db2.reshape(adapt),
        up2,
        ub2,
        g1,
        b1,
        g2,
        b2,
        r1.reshape(()),
        r2.reshape(()),
    )


def solution(mesh):
    split = P("dp", "seq", None)
    return jax.shard_map(
        per_device,
        mesh=mesh,
        in_specs=(split, split, P("dp", None)) + (P(),) * 16,
        out_specs=(split, split) + (P(),) * 14,
        check_vma=False,
    )
```
